32 devices in a mesh: req: 8 (over z, y), ctx: 4 (over x, core).
Axes of the slice: x: 2, y: 2, z: 4, core: 2. Of those that a mesh axis runs over, the one named last changes fastest.
Arguments:
- q_nope: bfloat16 [8, 128, 8192], P('req'), may hold values from -6 to 6
- q_rope: bfloat16 [8, 128, 4096], P('req'), may hold values from -600 to 600
- cache_latent: bfloat16 [8, 1024, 512], P('req', 'ctx'), may hold values from -6 to 6
- cache_rope: bfloat16 [8, 1024, 64], P('req', 'ctx'), may hold values from -4 to 4
- new_latent: bfloat16 [8, 128, 512], P('req', 'ctx'), may hold values from -6 to 6
- new_rope: bfloat16 [8, 128, 64], P('req', 'ctx'), may hold values from -8 to 8
- lengths: int32 [8, 4], P('req', 'ctx'), may hold values from 64 to 256, as said below
- w_key: bfloat16 [512, 8192], P(None, 'ctx'), may hold values from -0.25 to 0.25
- w_value: bfloat16 [512, 8192], P(None, 'ctx'), may hold values from -0.25 to 0.25
Outputs:
- attended: bfloat16 [8, 128, 8192], P('req', None, 'ctx')
The draws below stay inside these ranges and needn't reach their ends.
Inputs may be any that keep to these rules, and one draw needn't show every extreme that they name: lengths[r, g] counts the live cached rows at the start of request r's slots in context group g; all cached rows precede the new tokens; some entry equals 256 in every draw.
All inputs are finite; a program needn't handle non-finite values.
Results may differ from the reference program's by a relative error of at most 0.015.
Values may be sent and summed in bfloat16 or wider, within the bound.
No kernel may reach another device: no remote copies, remote signals or barrier semaphores. Data moves between devices by JAX's collectives and lax.ppermute only.
A program may use at most 128 MiB of HBM per device.

```python
import math
import jax
import jax.numpy as jnp
from jax import lax

DC = 512
DR = 64
DH = 128
DV = 128
HEADS = 64
Q_NEW = 128
ROWS_DEV = 256
REQS = 8
CTX_ROWS = 1024
N_CTX = 4


def rope_pair(key):
    base_key = jax.random.fold_in(key, 4242)
    key_query, key_fresh = jax.random.split(base_key, 2)
    query_draw = jnp.clip(jax.random.normal(key_query, (REQS, Q_NEW, HEADS * DR), jnp.float32), -4.0, 4.0)
    fresh_draw = jnp.clip(jax.random.normal(key_fresh, (REQS, Q_NEW, DR), jnp.float32), -4.0, 4.0)
    return (query_draw, fresh_draw)


def draw_q_rope(key, part):
    query_draw, fresh_draw = rope_pair(key)
    return query_draw.astype(jnp.bfloat16)


def draw_new_rope(key, part):
    query_draw, fresh_draw = rope_pair(key)
    return fresh_draw.astype(jnp.bfloat16)


def draw_lengths(key, part):
    key_draw, key_pick = jax.random.split(jax.random.fold_in(key, 31), 2)
    grid_shape = (REQS, N_CTX)
    lengths_flat = jax.random.randint(key_draw, grid_shape, ROWS_DEV // 4, ROWS_DEV + 1).reshape(-1)
    chosen = jax.random.randint(key_pick, (), 0, REQS * N_CTX)
    lengths_flat = jnp.where(jnp.arange(REQS * N_CTX) == chosen, ROWS_DEV, lengths_flat)
    return lengths_flat.reshape(grid_shape).astype(jnp.int32)


def level_of(key, extent, cuts, least, high):
    def one(dim, shards_of):
        heights = jax.random.uniform(jax.random.fold_in(jax.random.fold_in(key, 6), dim), (shards_of,), jnp.float32, least / len(cuts), high / len(cuts))
        return jnp.repeat(jnp.exp(heights), extent[dim] // shards_of).reshape((-1,) + (1,) * (len(extent) - dim - 1))

    loudness = one(*cuts[0])
    for cut in cuts[1:]:
        loudness = loudness * one(*cut)
    return loudness


def gaussian(key, shape, scale, limit, cuts=(), kind=jnp.bfloat16):
    factor_of = level_of(key, shape, cuts, -0.22, 0.18) if cuts else 1.0
    entries = jax.random.normal(key, shape, jnp.float32) * scale * factor_of
    return jnp.minimum(jnp.maximum(entries, -limit), limit).astype(kind)


def setup_inputs(seed: int = 0) -> dict:
    seeds = jax.random.split(jax.random.key(seed), 10)
    q_nope = gaussian(seeds[0], (REQS, Q_NEW, HEADS * DH), 1.0, 6.0, ((0, 8),))
    q_rope = draw_q_rope(jax.random.fold_in(seeds[9], 71), 0)
    cache_latent = gaussian(seeds[2], (REQS, CTX_ROWS, DC), 1.0, 6.0, ((0, 8), (1, 4)))
    cache_rope = gaussian(seeds[3], (REQS, CTX_ROWS, DR), 1.0, 4.0, ((0, 8), (1, 4)))
    new_latent = gaussian(seeds[4], (REQS, Q_NEW, DC), 1.0, 6.0, ((0, 8), (1, 4)))
    new_rope = draw_new_rope(jax.random.fold_in(seeds[9], 71), 0)
    lengths = draw_lengths(jax.random.fold_in(seeds[9], 71), 0)
    w_key = gaussian(seeds[7], (DC, HEADS * DH), DC ** -0.5, 0.25, ((1, 4),))
    w_value = gaussian(seeds[8], (DC, HEADS * DV), DC ** -0.5, 0.25, ((1, 4),))
    return {"q_nope": q_nope, "q_rope": q_rope, "cache_latent": cache_latent, "cache_rope": cache_rope, "new_latent": new_latent, "new_rope": new_rope, "lengths": lengths, "w_key": w_key, "w_value": w_value}


blocked_score = -1e+30

def reference(q_nope, q_rope, cache_latent, cache_rope, new_latent, new_rope, lengths, w_key, w_value):
    score_scale = 1.0 / math.sqrt(DH + DR)
    cached_count = ROWS_DEV * N_CTX
    local_rows = jnp.arange(cached_count, dtype=jnp.int32) % ROWS_DEV
    query_rows = jnp.arange(Q_NEW, dtype=jnp.int32)
    causal = query_rows[None, :] <= query_rows[:, None]

    def per_request(request_item):
        query_nope, query_rope, cache_rows, cache_keys, fresh_rows, fresh_keys, live_rows = request_item
        latent = jnp.concatenate([cache_rows, fresh_rows], axis=0)
        rope_keys = jnp.concatenate([cache_keys, fresh_keys], axis=0)
        total_rows = latent.shape[0]
        key_rows = jnp.dot(latent, w_key, preferred_element_type=jnp.float32).astype(jnp.bfloat16)
        value_rows = jnp.dot(latent, w_value, preferred_element_type=jnp.float32).astype(jnp.bfloat16)
        key_rows = lax.optimization_barrier(key_rows).astype(jnp.float32).reshape(total_rows, HEADS, DH)
        value_rows = lax.optimization_barrier(value_rows).astype(jnp.float32).reshape(total_rows, HEADS, DV)
        cached_ok = local_rows < jnp.repeat(live_rows, ROWS_DEV)
        visible = jnp.concatenate([jnp.broadcast_to(cached_ok[None, :], (Q_NEW, cached_count)), causal], axis=1)
        nope_part = query_nope.astype(jnp.float32).reshape(Q_NEW, HEADS, DH)
        rope_part = query_rope.astype(jnp.float32).reshape(Q_NEW, HEADS, DR)
        scores = jnp.einsum('qhd,khd->qhk', nope_part, key_rows)
        scores = scores + jnp.einsum('qhd,kd->qhk', rope_part, rope_keys.astype(jnp.float32))
        scores = jnp.where(visible[:, None, :], scores * score_scale, blocked_score)
        row_level = lax.optimization_barrier(jnp.max(scores, axis=-1, keepdims=True))
        weights = jnp.where(visible[:, None, :], jnp.exp(scores - row_level), 0.0)
        weight_sum = lax.optimization_barrier(jnp.sum(weights, axis=-1))
        rounded = lax.optimization_barrier(weights.astype(jnp.bfloat16)).astype(jnp.float32)
        numerator = jnp.einsum('qhk,khd->qhd', rounded, value_rows)
        return (numerator / weight_sum[..., None]).reshape(Q_NEW, HEADS * DV).astype(jnp.bfloat16)
    return lax.map(per_request, (q_nope, q_rope, cache_latent, cache_rope, new_latent, new_rope, lengths))
```

```python
import functools
import math

import jax
import jax.numpy as jnp
from jax import lax
from jax.experimental import pallas as pl
from jax.experimental.pallas import tpu as pltpu
from jax.sharding import PartitionSpec as P

DC = 512
DR = 64
DH = 128
DV = 128
HEADS = 64
LANES = 128
BLOCKED = -1e30
EXP_SCALE = math.log2(math.e) / math.sqrt(DH + DR)
HEADS_STEP = 4
VMEM_LIMIT = 28 * 1024 * 1024
BF16 = jnp.bfloat16
F32 = jnp.float32

VMEM = pl.BlockSpec(memory_space=pltpu.VMEM)
ANYWHERE = pl.BlockSpec(memory_space=pl.ANY)


def iota(shape, dim):
    return lax.broadcasted_iota(jnp.int32, shape, dim)


def params():
    return pltpu.CompilerParams(vmem_limit_bytes=VMEM_LIMIT)


def dot(a, b):
    return jnp.dot(a, b, preferred_element_type=F32)


def dot_t(a, b):
    return lax.dot_general(a, b, (((1,), (1,)), ((), ())), preferred_element_type=F32)


def pack_kernel(rope_ref, length_ref, out_ref):
    half = rope_ref.shape[0] // 2
    out_ref[:half, :DR] = rope_ref[:half, :]
    out_ref[:half, DR:] = rope_ref[half:, :]
    tail = out_ref.shape[0] - half
    out_ref[half:, :] = jnp.full((tail, LANES), length_ref[0, 0], jnp.int32).astype(F32).astype(BF16)


def pack(rope, length):
    half = rope.shape[0] // 2
    return pl.pallas_call(
        pack_kernel,
        out_shape=jax.ShapeDtypeStruct((half + 16, LANES), BF16),
        in_specs=[VMEM, pl.BlockSpec(memory_space=pltpu.SMEM)],
        out_specs=VMEM,
        compiler_params=params(),
        name="pack_rope",
    )(rope, length)


def queries_kernel(q_hbm, r_hbm, w_hbm, lat_ref, ext_ref, q_buf, r_buf, w_buf, sems):
    heads = lat_ref.shape[0] // q_buf.shape[0]
    count = q_buf.shape[0]
    me = lax.axis_index("ctx")
    q_first = pl.multiple_of(me * (heads * DH), LANES)
    r_first = pl.multiple_of(me * (heads * DR), LANES)
    steps = heads // HEADS_STEP
    width = HEADS_STEP * DH
    q_copy = pltpu.make_async_copy(q_hbm.at[0, :, pl.ds(q_first, heads * DH)], q_buf, sems.at[0])
    r_copy = pltpu.make_async_copy(r_hbm.at[0, :, pl.ds(r_first, heads * DR)], r_buf, sems.at[1])
    q_copy.start()
    w_copies = []
    for step in range(steps):
        cols = pl.ds(step * width, width)
        copy = pltpu.make_async_copy(w_hbm.at[:, cols], w_buf.at[:, cols], sems.at[2 + step])
        copy.start()
        w_copies.append(copy)
    r_copy.start()
    q_copy.wait()
    for step in range(steps):
        w_copies[step].wait()
        for head in range(step * HEADS_STEP, (step + 1) * HEADS_STEP):
            cols = slice(head * DH, (head + 1) * DH)
            lat_ref[head * count : (head + 1) * count, :] = dot_t(q_buf[:, cols], w_buf[:, cols]).astype(BF16)
    r_copy.wait()
    lane = iota((count, LANES), 1)
    side = jnp.where(lane == DR, 1.0, 0.0)
    for pair in range(heads // 2):
        both = r_buf[:, pair * LANES : (pair + 1) * LANES].astype(F32)
        for odd in range(2):
            one = pltpu.roll(both, DR, 1) if odd else both
            head = 2 * pair + odd
            ext_ref[head * count : (head + 1) * count, :] = jnp.where(lane < DR, one, side).astype(BF16)


def make_queries(q_nope, q_rope, w_key):
    count = q_nope.shape[1]
    heads = w_key.shape[1] // DH
    rows = heads * count
    return pl.pallas_call(
        queries_kernel,
        out_shape=(pltpu.VMEM((rows, DC), BF16), pltpu.VMEM((rows, LANES), BF16)),
        in_specs=[ANYWHERE, ANYWHERE, ANYWHERE],
        out_specs=(VMEM, VMEM),
        scratch_shapes=[
            pltpu.VMEM((count, heads * DH), BF16),
            pltpu.VMEM((count, heads * DR), BF16),
            pltpu.VMEM((DC, heads * DH), BF16),
            pltpu.SemaphoreType.DMA((2 + heads // HEADS_STEP,)),
        ],
        compiler_params=params(),
        cost_estimate=pl.CostEstimate(
            flops=2 * rows * DH * DC, bytes_accessed=2 * (DC * heads * DH + rows * (DH + DR)), transcendentals=0
        ),
        name="latent_queries",
    )(q_nope, q_rope, w_key)


def masked_rope(packed, slots):
    half = slots // 2
    lane = iota((half, LANES), 1)
    row = iota((half, LANES), 0).astype(F32)
    both = packed[:half, :].astype(F32)
    live = packed[half : half + 1, :].astype(F32)
    parts = []
    for part in range(2):
        one = pltpu.roll(both, DR, 1) if part else both
        blocked = jnp.where(row + part * half < live, 0.0, BLOCKED)
        parts.append(jnp.where(lane < DR, one, jnp.where(lane == DR, blocked, 0.0)).astype(BF16))
    return jnp.concatenate(parts, axis=0)


def first_kernel(latq_ref, extq_ref, *refs, blocks, cached):
    cache_refs, pack_refs = refs[:cached], refs[cached : 2 * cached]
    fresh_refs = refs[2 * cached : 2 * cached + blocks]
    rope_refs = refs[2 * cached + blocks : 2 * cached + 2 * blocks]
    acc_ref, sum_ref, max_ref, lat_buf, ext_buf, flat_buf, fext_buf = refs[2 * cached + 2 * blocks :]
    slots = cache_refs[0].shape[0]
    part = fresh_refs[0].shape[0]
    count = part * blocks
    for k in range(cached):
        lat_buf[k * slots : (k + 1) * slots, :] = cache_refs[k][...]
        ext_buf[k * slots : (k + 1) * slots, :] = masked_rope(pack_refs[k], slots)
    for k in range(blocks):
        flat_buf[k * part : (k + 1) * part, :] = fresh_refs[k][...]
        fext_buf[k * part : (k + 1) * part, :] = jnp.concatenate(
            [rope_refs[k][...], jnp.zeros((part, LANES - DR), BF16)], axis=1
        )
    me = lax.axis_index("ctx")
    col = iota((count, count), 1)
    origin = jnp.bitwise_xor(jnp.full((count, count), me, jnp.int32), col // part)
    bias = jnp.where(origin * part + col % part <= iota((count, count), 0), 0.0, BLOCKED)
    size = HEADS_STEP * count
    bias = jnp.concatenate([bias] * HEADS_STEP, axis=0)
    for step in range(latq_ref.shape[0] // size):
        rows = slice(step * size, (step + 1) * size)
        latq, extq = latq_ref[rows, :], extq_ref[rows, :]
        s_old = dot_t(latq, lat_buf[...]) + dot_t(extq, ext_buf[...])
        s_new = dot_t(latq, flat_buf[...]) + dot_t(extq, fext_buf[...]) + bias
        level = jnp.maximum(jnp.max(s_old, axis=1, keepdims=True), jnp.max(s_new, axis=1, keepdims=True))
        p_old = jnp.exp2((s_old - level) * EXP_SCALE)
        p_new = jnp.exp2((s_new - level) * EXP_SCALE)
        total = p_new[:, :LANES]
        for k in range(1, count // LANES):
            total = total + p_new[:, k * LANES : (k + 1) * LANES]
        for k in range(cached * slots // LANES):
            total = total + p_old[:, k * LANES : (k + 1) * LANES]
        acc_ref[rows, :] = dot(p_old.astype(BF16), lat_buf[...]) + dot(p_new.astype(BF16), flat_buf[...])
        sum_ref[rows, :] = total
        max_ref[rows, :] = jnp.broadcast_to(level, (size, LANES))


def state_shapes(rows):
    return (pltpu.VMEM((rows, DC), F32), pltpu.VMEM((rows, LANES), F32), pltpu.VMEM((rows, LANES), F32))


def first_pass(lat_q, ext_q, caches, packs, fresh, ropes):
    rows = lat_q.shape[0]
    cached, blocks = len(caches), len(fresh)
    slots = caches[0].shape[0]
    count = blocks * fresh[0].shape[0]
    keys = cached * slots + count
    return pl.pallas_call(
        functools.partial(first_kernel, blocks=blocks, cached=cached),
        out_shape=state_shapes(rows),
        in_specs=[VMEM] * (2 + 2 * cached + 2 * blocks),
        out_specs=(VMEM, VMEM, VMEM),
        scratch_shapes=[
            pltpu.VMEM((cached * slots, DC), BF16),
            pltpu.VMEM((cached * slots, LANES), BF16),
            pltpu.VMEM((count, DC), BF16),
            pltpu.VMEM((count, LANES), BF16),
        ],
        compiler_params=params(),
        cost_estimate=pl.CostEstimate(
            flops=2 * rows * keys * (2 * DC + DR), bytes_accessed=2 * keys * (DC + DR), transcendentals=rows * keys
        ),
        name="near_rows",
    )(lat_q, ext_q, *caches, *packs, *fresh, *ropes)


def advance(rows, latq_ref, extq_ref, lat_ref, ext, acc_ref, sum_ref, max_ref):
    lat = lat_ref[...]
    s = dot_t(latq_ref[rows, :], lat) + dot_t(extq_ref[rows, :], ext)
    before = max_ref[rows, :]
    level = jnp.maximum(before, jnp.max(s, axis=1, keepdims=True))
    factor = jnp.exp2((before - level) * EXP_SCALE)
    total = sum_ref[rows, :] * factor
    parts = []
    for k in range(lat.shape[0] // LANES):
        p = jnp.exp2((s[:, k * LANES : (k + 1) * LANES] - level) * EXP_SCALE)
        total = total + p
        parts.append(p.astype(BF16))
    grown = dot(jnp.concatenate(parts, axis=1), lat)
    return level, total, factor, grown


def scaled(acc, factor):
    return jnp.concatenate(
        [acc[:, k * LANES : (k + 1) * LANES] * factor for k in range(acc.shape[1] // LANES)], axis=1
    )


def middle_kernel(latq_ref, extq_ref, lat_ref, pack_ref, acc_in, sum_in, max_in, acc_ref, sum_ref, max_ref, *, size):
    ext = masked_rope(pack_ref, lat_ref.shape[0])
    for step in range(latq_ref.shape[0] // size):
        rows = slice(step * size, (step + 1) * size)
        level, total, factor, grown = advance(rows, latq_ref, extq_ref, lat_ref, ext, acc_in, sum_in, max_in)
        acc_ref[rows, :] = scaled(acc_in[rows, :], factor) + grown
        sum_ref[rows, :] = total
        max_ref[rows, :] = level


def attention_cost(rows, keys, more=0):
    return pl.CostEstimate(
        flops=2 * rows * keys * (2 * DC + DR) + more,
        bytes_accessed=2 * keys * (DC + DR) + more // 128,
        transcendentals=rows * keys,
    )


def middle_pass(lat_q, ext_q, lat, packed, state, count):
    rows = lat_q.shape[0]
    return pl.pallas_call(
        functools.partial(middle_kernel, size=HEADS_STEP * count),
        out_shape=state_shapes(rows),
        in_specs=[VMEM] * 7,
        out_specs=(VMEM, VMEM, VMEM),
        input_output_aliases={4: 0, 5: 1, 6: 2},
        compiler_params=params(),
        cost_estimate=attention_cost(rows, lat.shape[0]),
        name="far_rows",
    )(lat_q, ext_q, lat, packed, *state)


def last_kernel(latq_ref, extq_ref, lat_ref, pack_ref, acc_in, sum_in, max_in, w_hbm, out_ref, w_buf, sem, *, count):
    copy = pltpu.make_async_copy(w_hbm, w_buf, sem)
    copy.start()
    ext = masked_rope(pack_ref, lat_ref.shape[0])
    size = HEADS_STEP * count
    for step in range(latq_ref.shape[0] // size):
        rows = slice(step * size, (step + 1) * size)
        level, total, factor, grown = advance(rows, latq_ref, extq_ref, lat_ref, ext, acc_in, sum_in, max_in)
        whole = jnp.sum(total, axis=1, keepdims=True)
        mixed = ((scaled(acc_in[rows, :], factor) + grown) * (1.0 / whole)).astype(BF16)
        if step == 0:
            copy.wait()
        for k in range(HEADS_STEP):
            cols = slice((step * HEADS_STEP + k) * DV, (step * HEADS_STEP + k + 1) * DV)
            out_ref[:, cols] = dot(mixed[k * count : (k + 1) * count, :], w_buf[:, cols]).astype(BF16)


def last_pass(lat_q, ext_q, lat, packed, state, w_value, count):
    rows = lat_q.shape[0]
    return pl.pallas_call(
        functools.partial(last_kernel, count=count),
        out_shape=jax.ShapeDtypeStruct((count, w_value.shape[1]), BF16),
        in_specs=[VMEM] * 7 + [ANYWHERE],
        out_specs=VMEM,
        scratch_shapes=[pltpu.VMEM(w_value.shape, BF16), pltpu.SemaphoreType.DMA],
        compiler_params=params(),
        cost_estimate=attention_cost(rows, lat.shape[0], 2 * rows * DC * DV),
        name="last_rows",
    )(lat_q, ext_q, lat, packed, *state, w_value)


def hop(array, bit):
    size = lax.axis_size("ctx")
    return lax.ppermute(array, "ctx", [(k, k ^ bit) for k in range(size)])


def shards(q_nope, q_rope, cache_latent, cache_rope, new_latent, new_rope, lengths, w_key, w_value):
    count = q_nope.shape[1]
    cache, fresh, fresh_rope = cache_latent[0], new_latent[0], new_rope[0]
    packed = pack(cache_rope[0], lengths)

    fresh_all, rope_all = [fresh], [fresh_rope]
    far_fresh, far_rope, far_cache = hop(fresh, 2), hop(fresh_rope, 2), hop(cache, 2)
    far_pack = hop(packed, 2)
    near_cache, near_pack = hop(cache, 1), hop(packed, 1)
    fresh_all = [fresh, hop(fresh, 1), far_fresh, hop(far_fresh, 1)]
    rope_all = [fresh_rope, hop(fresh_rope, 1), far_rope, hop(far_rope, 1)]
    last_cache, last_pack = hop(far_cache, 1), hop(far_pack, 1)

    lat_q, ext_q = make_queries(q_nope, q_rope, w_key)
    state = first_pass(lat_q, ext_q, [cache, near_cache], [packed, near_pack], fresh_all, rope_all)
    state = middle_pass(lat_q, ext_q, far_cache, far_pack, state, count)
    return last_pass(lat_q, ext_q, last_cache, last_pack, state, w_value, count)[None]


def solution(mesh):
    return jax.shard_map(
        shards,
        mesh=mesh,
        in_specs=(
            P("req", None, None),
            P("req", None, None),
            P("req", "ctx", None),
            P("req", "ctx", None),
            P("req", "ctx", None),
            P("req", "ctx", None),
            P("req", "ctx"),
            P(None, "ctx"),
            P(None, "ctx"),
        ),
        out_specs=P("req", None, "ctx"),
        check_vma=False,
    )
```

```python
import functools
import math

import jax
import jax.numpy as jnp
from jax import lax
from jax.experimental import pallas as pl
from jax.experimental.pallas import tpu as pltpu
from jax.sharding import PartitionSpec as P

DC = 512
DR = 64
DH = 128
DV = 128
LANES = 128
KEY = DC + LANES
BLOCKED = -1e30
EXP_SCALE = math.log2(math.e) / math.sqrt(DH + DR)
HEADS_STEP = 4
GROUP = 16
COSTS = {"pack": 0.001, "latent_queries": 0.001, "pass_on": 0.001, "near_rows": 1.0, "far_rows": 3.0, "last_rows": 0.001}
VMEM_LIMIT = 20 * 1024 * 1024


def cost(micros):
    return pl.CostEstimate(flops=int(micros * 1e9), bytes_accessed=1024, transcendentals=0)


BF16 = jnp.bfloat16
F32 = jnp.float32

VMEM = pl.BlockSpec(memory_space=pltpu.VMEM)
HBM = pl.BlockSpec(memory_space=pltpu.HBM)
ANYWHERE = pl.BlockSpec(memory_space=pl.ANY)


def iota(shape, dim):
    return lax.broadcasted_iota(jnp.int32, shape, dim)


def params():
    return pltpu.CompilerParams(vmem_limit_bytes=VMEM_LIMIT)


def in_vmem(array):
    return pltpu.with_memory_space_constraint(array, pltpu.VMEM)


def dot(a, b):
    return jnp.dot(a, b, preferred_element_type=F32)


def dot_t(a, b):
    return lax.dot_general(a, b, (((1,), (1,)), ((), ())), preferred_element_type=F32)


def in_hbm(array):
    return pltpu.with_memory_space_constraint(array, pltpu.HBM)


def pack_kernel(fresh_hbm, rope_hbm, cached_hbm, length_ref, note_ref, rope_buf, cached_buf, sems):
    part = fresh_hbm.shape[0]
    slots = cached_hbm.shape[1]
    copies = [
        pltpu.make_async_copy(fresh_hbm, note_ref.at[:part, :], sems.at[0]),
        pltpu.make_async_copy(rope_hbm, rope_buf, sems.at[1]),
        pltpu.make_async_copy(cached_hbm, cached_buf, sems.at[2]),
    ]
    for copy in copies:
        copy.start()
    note_ref[part : part + GROUP, :] = jnp.zeros((GROUP, DC), BF16)
    groups = part // GROUP
    live = jnp.broadcast_to(length_ref[...], (GROUP, LANES)).astype(F32).astype(BF16)
    note_ref[part : part + GROUP, groups * LANES : (groups + 1) * LANES] = live
    copies[1].wait()
    for k in range(groups):
        note_ref[part : part + GROUP, k * LANES : k * LANES + DR] = rope_buf[k * GROUP : (k + 1) * GROUP, :]
    copies[2].wait()
    note_ref[part + GROUP :, :slots] = cached_buf[: DR // 2, :]
    note_ref[part + GROUP :, slots:] = cached_buf[DR // 2 :, :]
    copies[0].wait()


def pack(fresh, rope, cached_rope, length):
    part = fresh.shape[0]
    return pl.pallas_call(
        pack_kernel,
        out_shape=pltpu.VMEM((part + GROUP + DR // 2, DC), BF16),
        in_specs=[HBM, HBM, HBM, VMEM],
        out_specs=VMEM,
        scratch_shapes=[
            pltpu.VMEM(rope.shape, BF16),
            pltpu.VMEM(cached_rope.shape, BF16),
            pltpu.SemaphoreType.DMA((3,)),
        ],
        compiler_params=params(),
        cost_estimate=cost(COSTS["pack"]),
        name="pack",
    )(in_hbm(fresh), in_hbm(rope), in_hbm(cached_rope), length)


def queries_kernel(q_hbm, r_hbm, w_hbm, out_ref, q_buf, r_buf, w_buf, sems):
    count = q_buf.shape[0]
    heads = out_ref.shape[0] // count
    me = lax.axis_index("ctx")
    q_first = pl.multiple_of(me * (heads * DH), LANES)
    r_first = pl.multiple_of(me * (heads * DR), LANES)
    q_copy = pltpu.make_async_copy(q_hbm.at[0, :, pl.ds(q_first, heads * DH)], q_buf, sems.at[0])
    r_copy = pltpu.make_async_copy(r_hbm.at[0, :, pl.ds(r_first, heads * DR)], r_buf, sems.at[1])
    q_copy.start()
    width = HEADS_STEP * DH
    w_copies = []
    for step in range(heads // HEADS_STEP):
        cols = pl.ds(step * width, width)
        w_copies.append(pltpu.make_async_copy(w_hbm.at[:, cols], w_buf.at[:, cols], sems.at[2 + step]))
        w_copies[-1].start()
    r_copy.start()
    q_copy.wait()
    for head in range(heads):
        if head % HEADS_STEP == 0:
            w_copies[head // HEADS_STEP].wait()
        cols = slice(head * DH, (head + 1) * DH)
        out_ref[head * count : (head + 1) * count, :DC] = dot_t(q_buf[:, cols], w_buf[:, cols]).astype(BF16)
    r_copy.wait()
    lane = iota((count, LANES), 1)
    side = jnp.where(lane == DR, 1.0, 0.0)
    for pair in range(heads // 2):
        both = r_buf[:, pair * LANES : (pair + 1) * LANES].astype(F32)
        for odd in range(2):
            one = pltpu.roll(both, DR, 1) if odd else both
            head = 2 * pair + odd
            out_ref[head * count : (head + 1) * count, DC:] = jnp.where(lane < DR, one, side).astype(BF16)


def make_queries(q_nope, q_rope, w_key):
    count = q_nope.shape[1]
    heads = w_key.shape[1] // DH
    rows = heads * count
    return pl.pallas_call(
        queries_kernel,
        out_shape=pltpu.VMEM((rows, KEY), BF16),
        in_specs=[HBM, HBM, HBM],
        out_specs=VMEM,
        scratch_shapes=[
            pltpu.VMEM((count, heads * DH), BF16),
            pltpu.VMEM((count, heads * DR), BF16),
            pltpu.VMEM(w_key.shape, BF16),
            pltpu.SemaphoreType.DMA((2 + heads // HEADS_STEP,)),
        ],
        compiler_params=params(),
        cost_estimate=cost(COSTS["latent_queries"]),
        name="latent_queries",
    )(in_hbm(q_nope), in_hbm(q_rope), in_hbm(w_key))


def pass_kernel(array_ref, token_ref, out_ref):
    out_ref[...] = array_ref[...]


def after(array, token):
    return pl.pallas_call(
        pass_kernel,
        out_shape=pltpu.VMEM(array.shape, BF16),
        in_specs=[VMEM, ANYWHERE],
        out_specs=VMEM,
        compiler_params=params(),
        cost_estimate=cost(COSTS["pass_on"]),
        name="pass_on",
    )(array, token)


def put_cached(key_buf, first, lat_ref, note_ref):
    slots = lat_ref.shape[0]
    part = note_ref.shape[0] - GROUP - DR // 2
    lane = part // GROUP * LANES
    live = note_ref[part : part + 1, lane : lane + 1].astype(F32)
    blocked = jnp.where(iota((LANES - DR, slots), 1).astype(F32) < live, 0.0, BLOCKED)
    blocked = jnp.where(iota((LANES - DR, slots), 0) == 0, blocked, 0.0)
    rope = note_ref[part + GROUP :, :].astype(F32)
    both = jnp.concatenate([rope[:, :slots], rope[:, slots:], blocked], axis=0)
    key_buf[first : first + slots, :DC] = lat_ref[...]
    key_buf[first : first + slots, DC:] = both.T.astype(BF16)


def put_fresh(key_buf, first, note_refs):
    part = note_refs[0].shape[0] - GROUP - DR // 2
    for index, note_ref in enumerate(note_refs):
        key_buf[first + index * part : first + (index + 1) * part, :DC] = note_ref[:part, :]
        for k in range(part // GROUP):
            rows = span(k, GROUP, first + index * part)
            key_buf[rows, DC:] = note_ref[part : part + GROUP, k * LANES : (k + 1) * LANES]


def causal(part, blocks):
    count = part * blocks
    me = lax.axis_index("ctx")
    col = iota((count, count), 1)
    origin = jnp.bitwise_xor(jnp.full((count, count), me, jnp.int32), col // part)
    return jnp.where(origin * part + col % part <= iota((count, count), 0), 0.0, BLOCKED)


def pipeline(steps, scores, weigh, collect):
    upcoming, previous = scores(0), None
    for step in range(steps):
        now = upcoming
        if step + 1 < steps:
            upcoming = scores(step + 1)
        if previous is not None:
            collect(step - 1, *previous)
        previous = weigh(step, now)
    collect(steps - 1, *previous)


def exponents(s, level, total):
    parts = []
    for k in range(s.shape[1] // LANES):
        p = jnp.exp2((s[:, k * LANES : (k + 1) * LANES] - level) * EXP_SCALE)
        total = p if total is None else total + p
        parts.append(p.astype(BF16))
    return jnp.concatenate(parts, axis=1), total


def span(step, size, first=0):
    return slice(first + step * size, first + (step + 1) * size)


def state_shapes(rows):
    return (pltpu.VMEM((rows, DC), F32), pltpu.VMEM((rows, LANES), F32), pltpu.VMEM((rows, LANES), F32))


def near_kernel(q_ref, *refs, cached, size):
    acc_ref, sum_ref, max_ref, key_buf = refs[2 * cached :]
    slots = refs[0].shape[0]
    for k in range(cached):
        put_cached(key_buf, k * slots, refs[2 * k], refs[2 * k + 1])

    def scores(step):
        return dot_t(q_ref[span(step, size), :], key_buf[...])

    def weigh(step, s):
        level = jnp.max(s, axis=1, keepdims=True)
        p, total = exponents(s, level, None)
        sum_ref[span(step, size), :] = total
        max_ref[span(step, size), :] = jnp.broadcast_to(level, (size, LANES))
        return (p,)

    def collect(step, p):
        acc_ref[span(step, size), :] = dot(p, key_buf[:, :DC])

    pipeline(q_ref.shape[0] // size, scores, weigh, collect)


def near_pass(q, blocks, count):
    rows = q.shape[0]
    keys = sum(block[0].shape[0] for block in blocks)
    return pl.pallas_call(
        functools.partial(near_kernel, cached=len(blocks), size=HEADS_STEP * count),
        out_shape=state_shapes(rows),
        in_specs=[VMEM] * (1 + 2 * len(blocks)),
        out_specs=(VMEM, VMEM, VMEM),
        scratch_shapes=[pltpu.VMEM((keys, KEY), BF16)],
        compiler_params=params(),
        cost_estimate=cost(COSTS["near_rows"]),
        name="near_rows",
    )(q, *[array for block in blocks for array in block])


def advance(q_ref, key_buf, state_in, state_out, size):
    acc_in, sum_in, max_in = state_in
    acc_ref, sum_ref, max_ref = state_out

    def scores(step):
        return dot_t(q_ref[span(step, size), :], key_buf[...])

    def weigh(step, s):
        rows = span(step, size)
        before = max_in[rows, :]
        level = jnp.maximum(before, jnp.max(s, axis=1, keepdims=True))
        factor = jnp.exp2((before - level) * EXP_SCALE)
        p, total = exponents(s, level, sum_in[rows, :] * factor)
        sum_ref[rows, :] = total
        max_ref[rows, :] = level
        return p, factor

    def collect(step, p, factor):
        rows = span(step, size)
        grown = dot(p, key_buf[:, :DC])
        for k in range(DC // LANES):
            cols = slice(k * LANES, (k + 1) * LANES)
            acc_ref[rows, cols] = acc_in[rows, cols] * factor + grown[:, cols]

    pipeline(q_ref.shape[0] // size, scores, weigh, collect)


def far_kernel(q_ref, lat_ref, note_ref, *refs, size):
    put_cached(refs[6], 0, lat_ref, note_ref)
    advance(q_ref, refs[6], refs[:3], refs[3:6], size)


def far_pass(q, lat, note, state, count):
    rows = q.shape[0]
    return pl.pallas_call(
        functools.partial(far_kernel, size=HEADS_STEP * count),
        out_shape=state_shapes(rows),
        in_specs=[VMEM] * 6,
        out_specs=(VMEM, VMEM, VMEM),
        scratch_shapes=[pltpu.VMEM((lat.shape[0], KEY), BF16)],
        compiler_params=params(),
        cost_estimate=cost(COSTS["far_rows"]),
        name="far_rows",
    )(q, lat, note, *state)


def last_kernel(q_ref, lat_ref, *refs, blocks, size):
    notes, refs = refs[:blocks], refs[blocks:]
    acc_in, sum_in, max_in, w_ref, out_ref, key_buf = refs
    slots = lat_ref.shape[0]
    count = out_ref.shape[0]
    put_cached(key_buf, 0, lat_ref, notes[-1])
    put_fresh(key_buf, slots, notes)
    bias = jnp.concatenate([causal(count // blocks, blocks)] * HEADS_STEP, axis=0)

    def scores(step):
        return dot_t(q_ref[span(step, size), :], key_buf[...])

    def weigh(step, s):
        rows = span(step, size)
        s = jnp.concatenate([s[:, :slots], s[:, slots:] + bias], axis=1)
        before = max_in[rows, :]
        level = jnp.maximum(before, jnp.max(s, axis=1, keepdims=True))
        factor = jnp.exp2((before - level) * EXP_SCALE)
        p, total = exponents(s, level, sum_in[rows, :] * factor)
        inverse = 1.0 / jnp.sum(total, axis=1, keepdims=True)
        return p, factor * inverse, inverse

    def collect(step, p, factor, inverse):
        rows = span(step, size)
        grown = dot(p, key_buf[:, :DC])
        mixed = []
        for k in range(DC // LANES):
            cols = slice(k * LANES, (k + 1) * LANES)
            mixed.append((acc_in[rows, cols] * factor + grown[:, cols] * inverse).astype(BF16))
        mixed = jnp.concatenate(mixed, axis=1)
        for k in range(HEADS_STEP):
            cols = span(step * HEADS_STEP + k, DV)
            out_ref[:, cols] = dot(mixed[span(k, count), :], w_ref[:, cols]).astype(BF16)

    pipeline(q_ref.shape[0] // size, scores, weigh, collect)


def last_pass(q, lat, notes, state, w_value, count):
    rows = q.shape[0]
    return pl.pallas_call(
        functools.partial(last_kernel, blocks=len(notes), size=HEADS_STEP * count),
        out_shape=jax.ShapeDtypeStruct((count, w_value.shape[1]), BF16),
        in_specs=[VMEM] * (6 + len(notes)),
        out_specs=VMEM,
        scratch_shapes=[pltpu.VMEM((lat.shape[0] + count, KEY), BF16)],
        compiler_params=params(),
        cost_estimate=cost(COSTS["last_rows"]),
        name="last_rows",
    )(q, lat, *notes, *state, in_vmem(w_value))


def hop(array, bit):
    size = lax.axis_size("ctx")
    return lax.ppermute(array, "ctx", [(k, k ^ bit) for k in range(size)])


def shards(q_nope, q_rope, cache_latent, cache_rope, new_latent, new_rope, lengths, w_key, w_value):
    count = q_nope.shape[1]
    lat = cache_latent[0]
    far_lat, near_lat = hop(lat, 2), hop(lat, 1)
    note = pack(new_latent[0], new_rope[0], cache_rope[0].T, lengths)
    near_note = hop(note, 1)
    q = make_queries(q_nope, q_rope, w_key)
    far_note = hop(after(note, q), 2)
    state = near_pass(q, [(lat, note), (near_lat, near_note)], count)
    last_lat = hop(after(far_lat, state[2]), 1)
    last_note = hop(after(far_note, state[2]), 1)
    state = far_pass(q, far_lat, far_note, state, count)
    return last_pass(q, last_lat, [note, near_note, far_note, last_note], state, w_value, count)[None]


def solution(mesh):
    return jax.shard_map(
        shards,
        mesh=mesh,
        in_specs=(
            P("req", None, None),
            P("req", None, None),
            P("req", "ctx", None),
            P("req", "ctx", None),
            P("req", "ctx", None),
            P("req", "ctx", None),
            P("req", "ctx"),
            P(None, "ctx"),
            P(None, "ctx"),
        ),
        out_specs=P("req", None, "ctx"),
        check_vma=False,
    )
```

```python
import functools
import math

import jax
import jax.numpy as jnp
from jax import lax
from jax.experimental import pallas as pl
from jax.experimental.pallas import tpu as pltpu
from jax.sharding import PartitionSpec as P

DC = 512
DR = 64
DH = 128
DV = 128
LANES = 128
KEY = DC + LANES
BLOCKED = -1e30
EXP_SCALE = math.log2(math.e) / math.sqrt(DH + DR)
HEADS_STEP = 4
GROUP = 16
COSTS = {"prepare": 0.001, "pass_on": 0.001, "near_rows": 1.0, "lat_scores": 1.0, "far_rows": 3.0, "last_rows": 0.001}
VMEM_LIMIT = 20 * 1024 * 1024


def cost(micros):
    return pl.CostEstimate(flops=int(micros * 1e9), bytes_accessed=1024, transcendentals=0)


BF16 = jnp.bfloat16
F32 = jnp.float32

VMEM = pl.BlockSpec(memory_space=pltpu.VMEM)
HBM = pl.BlockSpec(memory_space=pltpu.HBM)
ANYWHERE = pl.BlockSpec(memory_space=pl.ANY)


def iota(shape, dim):
    return lax.broadcasted_iota(jnp.int32, shape, dim)


def span(step, size, first=0):
    return slice(first + step * size, first + (step + 1) * size)


def params():
    return pltpu.CompilerParams(vmem_limit_bytes=VMEM_LIMIT)


def in_vmem(array):
    return pltpu.with_memory_space_constraint(array, pltpu.VMEM)


def dot(a, b):
    return jnp.dot(a, b, preferred_element_type=F32)


def dot_t(a, b):
    return lax.dot_general(a, b, (((1,), (1,)), ((), ())), preferred_element_type=F32)


def in_hbm(array):
    return pltpu.with_memory_space_constraint(array, pltpu.HBM)


def prepare_kernel(
    q_hbm,
    r_hbm,
    w_hbm,
    lat_hbm,
    fresh_hbm,
    rope_hbm,
    cached_hbm,
    length_ref,
    note_ref,
    out_ref,
    lat_ref,
    q_buf,
    r_buf,
    w_buf,
    rope_buf,
    cached_buf,
    sems,
):
    part = fresh_hbm.shape[0]
    slots = cached_hbm.shape[1]
    count = q_buf.shape[0]
    heads = out_ref.shape[0] // count
    me = lax.axis_index("ctx")
    q_first = pl.multiple_of(me * (heads * DH), LANES)
    r_first = pl.multiple_of(me * (heads * DR), LANES)
    width = HEADS_STEP * DH
    pairs = [
        (q_hbm.at[0, :, pl.ds(q_first, heads * DH)], q_buf),
        (fresh_hbm, note_ref.at[:part, :]),
        (rope_hbm, rope_buf),
        (cached_hbm, cached_buf),
        (r_hbm.at[0, :, pl.ds(r_first, heads * DR)], r_buf),
    ]
    for step in range(heads // HEADS_STEP):
        cols = pl.ds(step * width, width)
        pairs.append((w_hbm.at[:, cols], w_buf.at[:, cols]))
    pairs.append((lat_hbm, lat_ref))
    copies = [pltpu.make_async_copy(source, target, sems.at[k]) for k, (source, target) in enumerate(pairs)]
    for copy in copies:
        copy.start()
    q_copy, fresh_copy, rope_copy, cached_copy, r_copy = copies[:5]
    w_copies, lat_copy = copies[5:-1], copies[-1]

    groups = part // GROUP
    note_ref[part : part + GROUP, :] = jnp.zeros((GROUP, DC), BF16)
    live = jnp.broadcast_to(length_ref[...], (GROUP, LANES)).astype(F32).astype(BF16)
    note_ref[part : part + GROUP, groups * LANES : (groups + 1) * LANES] = live
    rope_copy.wait()
    for k in range(groups):
        note_ref[part : part + GROUP, k * LANES : k * LANES + DR] = rope_buf[k * GROUP : (k + 1) * GROUP, :]
    cached_copy.wait()
    note_ref[part + GROUP :, :slots] = cached_buf[: DR // 2, :]
    note_ref[part + GROUP :, slots:] = cached_buf[DR // 2 :, :]

    r_copy.wait()
    lane = iota((count, LANES), 1)
    side = jnp.where(lane == DR, 1.0, 0.0)
    for pair in range(heads // 2):
        both = r_buf[:, pair * LANES : (pair + 1) * LANES].astype(F32)
        for odd in range(2):
            one = pltpu.roll(both, DR, 1) if odd else both
            out_ref[span(2 * pair + odd, count), DC:] = jnp.where(lane < DR, one, side).astype(BF16)
    q_copy.wait()
    for head in range(heads):
        if head % HEADS_STEP == 0:
            w_copies[head // HEADS_STEP].wait()
        cols = span(head, DH)
        out_ref[span(head, count), :DC] = dot_t(q_buf[:, cols], w_buf[:, cols]).astype(BF16)
    fresh_copy.wait()
    lat_copy.wait()


def prepare(q_nope, q_rope, w_key, lat, fresh, rope, cached_rope, length):
    count = q_nope.shape[1]
    heads = w_key.shape[1] // DH
    part = fresh.shape[0]
    return pl.pallas_call(
        prepare_kernel,
        out_shape=(
            pltpu.VMEM((part + GROUP + DR // 2, DC), BF16),
            pltpu.VMEM((heads * count, KEY), BF16),
            pltpu.VMEM(lat.shape, BF16),
        ),
        in_specs=[HBM] * 7 + [VMEM],
        out_specs=(VMEM, VMEM, VMEM),
        scratch_shapes=[
            pltpu.VMEM((count, heads * DH), BF16),
            pltpu.VMEM((count, heads * DR), BF16),
            pltpu.VMEM(w_key.shape, BF16),
            pltpu.VMEM(rope.shape, BF16),
            pltpu.VMEM(cached_rope.shape, BF16),
            pltpu.SemaphoreType.DMA((6 + heads // HEADS_STEP,)),
        ],
        compiler_params=params(),
        cost_estimate=cost(COSTS["prepare"]),
        name="prepare",
    )(*[in_hbm(array) for array in (q_nope, q_rope, w_key, lat, fresh, rope, cached_rope)], length)


def pass_kernel(array_ref, token_ref, out_ref):
    out_ref[...] = array_ref[...]


def after(array, token):
    return pl.pallas_call(
        pass_kernel,
        out_shape=pltpu.VMEM(array.shape, BF16),
        in_specs=[VMEM, ANYWHERE],
        out_specs=VMEM,
        compiler_params=params(),
        cost_estimate=cost(COSTS["pass_on"]),
        name="pass_on",
    )(array, token)


def put_cached(key_buf, first, lat_ref, note_ref):
    slots = lat_ref.shape[0]
    key_buf[first : first + slots, :DC] = lat_ref[...]
    key_buf[first : first + slots, DC:] = masked_rope(note_ref, slots)


def masked_rope(note_ref, slots):
    part = note_ref.shape[0] - GROUP - DR // 2
    lane = part // GROUP * LANES
    live = note_ref[part : part + 1, lane : lane + 1].astype(F32)
    blocked = jnp.where(iota((LANES - DR, slots), 1).astype(F32) < live, 0.0, BLOCKED)
    blocked = jnp.where(iota((LANES - DR, slots), 0) == 0, blocked, 0.0)
    rope = note_ref[part + GROUP :, :].astype(F32)
    return jnp.concatenate([rope[:, :slots], rope[:, slots:], blocked], axis=0).T.astype(BF16)


def put_fresh(key_buf, first, note_refs):
    part = note_refs[0].shape[0] - GROUP - DR // 2
    for index, note_ref in enumerate(note_refs):
        key_buf[first + index * part : first + (index + 1) * part, :DC] = note_ref[:part, :]
        for k in range(part // GROUP):
            rows = span(k, GROUP, first + index * part)
            key_buf[rows, DC:] = note_ref[part : part + GROUP, k * LANES : (k + 1) * LANES]


def causal(part, blocks):
    count = part * blocks
    me = lax.axis_index("ctx")
    col = iota((count, count), 1)
    origin = jnp.bitwise_xor(jnp.full((count, count), me, jnp.int32), col // part)
    return jnp.where(origin * part + col % part <= iota((count, count), 0), 0.0, BLOCKED)


def pipeline(steps, scores, weigh, collect):
    upcoming, previous = scores(0), None
    for step in range(steps):
        now = upcoming
        if step + 1 < steps:
            upcoming = scores(step + 1)
        if previous is not None:
            collect(step - 1, *previous)
        previous = weigh(step, now)
    collect(steps - 1, *previous)


def exponents(s, level, total):
    parts = []
    for k in range(s.shape[1] // LANES):
        p = jnp.exp2((s[:, k * LANES : (k + 1) * LANES] - level) * EXP_SCALE)
        total = p if total is None else total + p
        parts.append(p.astype(BF16))
    return jnp.concatenate(parts, axis=1), total


def state_shapes(rows):
    return (pltpu.VMEM((rows, DC), F32), pltpu.VMEM((rows, LANES), F32), pltpu.VMEM((rows, LANES), F32))


def near_kernel(q_ref, *refs, cached, size):
    acc_ref, sum_ref, max_ref, key_buf = refs[2 * cached :]
    slots = refs[0].shape[0]
    for k in range(cached):
        put_cached(key_buf, k * slots, refs[2 * k], refs[2 * k + 1])

    def scores(step):
        return dot_t(q_ref[span(step, size), :], key_buf[...])

    def weigh(step, s):
        level = jnp.max(s, axis=1, keepdims=True)
        p, total = exponents(s, level, None)
        sum_ref[span(step, size), :] = total
        max_ref[span(step, size), :] = jnp.broadcast_to(level, (size, LANES))
        return (p,)

    def collect(step, p):
        acc_ref[span(step, size), :] = dot(p, key_buf[:, :DC])

    pipeline(q_ref.shape[0] // size, scores, weigh, collect)


def near_pass(q, blocks, count):
    rows = q.shape[0]
    keys = sum(block[0].shape[0] for block in blocks)
    return pl.pallas_call(
        functools.partial(near_kernel, cached=len(blocks), size=HEADS_STEP * count),
        out_shape=state_shapes(rows),
        in_specs=[VMEM] * (1 + 2 * len(blocks)),
        out_specs=(VMEM, VMEM, VMEM),
        scratch_shapes=[pltpu.VMEM((keys, KEY), BF16)],
        compiler_params=params(),
        cost_estimate=cost(COSTS["near_rows"]),
        name="near_rows",
    )(q, *[array for block in blocks for array in block])


def scores_kernel(q_ref, lat_ref, out_ref, *, size):
    for step in range(q_ref.shape[0] // size):
        rows = span(step, size)
        out_ref[rows, :] = dot_t(q_ref[rows, :DC], lat_ref[...])


def lat_scores(q, lat, count):
    rows = q.shape[0]
    return pl.pallas_call(
        functools.partial(scores_kernel, size=HEADS_STEP * count),
        out_shape=pltpu.VMEM((rows, lat.shape[0]), F32),
        in_specs=[VMEM] * 2,
        out_specs=VMEM,
        compiler_params=params(),
        cost_estimate=cost(COSTS["lat_scores"]),
        name="lat_scores",
    )(q, lat)


def far_kernel(q_ref, lat_ref, note_ref, s_ref, acc_in, sum_in, max_in, acc_ref, sum_ref, max_ref, ext_buf, *, size):
    ext_buf[...] = masked_rope(note_ref, lat_ref.shape[0])

    def scores(step):
        rows = span(step, size)
        return s_ref[rows, :] + dot_t(q_ref[rows, DC:], ext_buf[...])

    def weigh(step, s):
        rows = span(step, size)
        before = max_in[rows, :]
        level = jnp.maximum(before, jnp.max(s, axis=1, keepdims=True))
        factor = jnp.exp2((before - level) * EXP_SCALE)
        p, total = exponents(s, level, sum_in[rows, :] * factor)
        sum_ref[rows, :] = total
        max_ref[rows, :] = level
        return p, factor

    def collect(step, p, factor):
        rows = span(step, size)
        grown = dot(p, lat_ref[...])
        for k in range(DC // LANES):
            cols = span(k, LANES)
            acc_ref[rows, cols] = acc_in[rows, cols] * factor + grown[:, cols]

    pipeline(q_ref.shape[0] // size, scores, weigh, collect)


def far_pass(q, lat, note, lat_part, state, count):
    rows = q.shape[0]
    return pl.pallas_call(
        functools.partial(far_kernel, size=HEADS_STEP * count),
        out_shape=state_shapes(rows),
        in_specs=[VMEM] * 7,
        out_specs=(VMEM, VMEM, VMEM),
        scratch_shapes=[pltpu.VMEM((lat.shape[0], LANES), BF16)],
        compiler_params=params(),
        cost_estimate=cost(COSTS["far_rows"]),
        name="far_rows",
    )(q, lat, note, lat_part, *state)


def last_kernel(q_ref, lat_ref, *refs, blocks, size):
    notes, refs = refs[:blocks], refs[blocks:]
    acc_in, sum_in, max_in, w_ref, out_ref, key_buf = refs
    slots = lat_ref.shape[0]
    count = out_ref.shape[0]
    put_cached(key_buf, 0, lat_ref, notes[-1])
    put_fresh(key_buf, slots, notes)
    bias = jnp.concatenate([causal(count // blocks, blocks)] * HEADS_STEP, axis=0)

    def scores(step):
        s = dot_t(q_ref[span(step, size), :], key_buf[...])
        return jnp.concatenate([s[:, :slots], s[:, slots:] + bias], axis=1)

    def weigh(step, s):
        rows = span(step, size)
        before = max_in[rows, :]
        level = jnp.maximum(before, jnp.max(s, axis=1, keepdims=True))
        factor = jnp.exp2((before - level) * EXP_SCALE)
        p, total = exponents(s, level, sum_in[rows, :] * factor)
        inverse = 1.0 / jnp.sum(total, axis=1, keepdims=True)
        return p, factor * inverse, inverse

    def collect(step, p, factor, inverse):
        rows = span(step, size)
        grown = dot(p, key_buf[:, :DC])
        mixed = []
        for k in range(DC // LANES):
            cols = slice(k * LANES, (k + 1) * LANES)
            mixed.append((acc_in[rows, cols] * factor + grown[:, cols] * inverse).astype(BF16))
        mixed = jnp.concatenate(mixed, axis=1)
        for k in range(HEADS_STEP):
            cols = span(step * HEADS_STEP + k, DV)
            out_ref[:, cols] = dot(mixed[span(k, count), :], w_ref[:, cols]).astype(BF16)

    pipeline(q_ref.shape[0] // size, scores, weigh, collect)


def last_pass(q, lat, notes, state, w_value, count):
    rows = q.shape[0]
    return pl.pallas_call(
        functools.partial(last_kernel, blocks=len(notes), size=HEADS_STEP * count),
        out_shape=jax.ShapeDtypeStruct((count, w_value.shape[1]), BF16),
        in_specs=[VMEM] * (6 + len(notes)),
        out_specs=VMEM,
        scratch_shapes=[pltpu.VMEM((lat.shape[0] + count, KEY), BF16)],
        compiler_params=params(),
        cost_estimate=cost(COSTS["last_rows"]),
        name="last_rows",
    )(q, lat, *notes, *state, in_vmem(w_value))


def hop(array, bit):
    size = lax.axis_size("ctx")
    return lax.ppermute(array, "ctx", [(k, k ^ bit) for k in range(size)])


def shards(q_nope, q_rope, cache_latent, cache_rope, new_latent, new_rope, lengths, w_key, w_value):
    count = q_nope.shape[1]
    lat = cache_latent[0]
    far_lat, near_lat = hop(lat, 2), hop(lat, 1)
    note, q, lat = prepare(
        q_nope, q_rope, w_key, lat, new_latent[0], new_rope[0], cache_rope[0].T, lengths
    )
    far_note, near_note = hop(note, 2), hop(note, 1)
    state = near_pass(q, [(lat, note), (near_lat, near_note)], count)
    last_lat = hop(after(far_lat, state[2]), 1)
    far_part = lat_scores(q, far_lat, count)
    last_note = hop(after(far_note, far_part), 1)
    state = far_pass(q, far_lat, far_note, far_part, state, count)
    notes = [note, near_note, far_note, last_note]
    return last_pass(q, last_lat, notes, state, w_value, count)[None]


def solution(mesh):
    return jax.shard_map(
        shards,
        mesh=mesh,
        in_specs=(
            P("req", None, None),
            P("req", None, None),
            P("req", "ctx", None),
            P("req", "ctx", None),
            P("req", "ctx", None),
            P("req", "ctx", None),
            P("req", "ctx"),
            P(None, "ctx"),
            P(None, "ctx"),
        ),
        out_specs=P("req", None, "ctx"),
        check_vma=False,
    )
```

```python
import functools
import math

import jax
import jax.numpy as jnp
from jax import lax
from jax.experimental import pallas as pl
from jax.experimental.pallas import tpu as pltpu
from jax.sharding import PartitionSpec as P

DC = 512
DR = 64
DH = 128
DV = 128
LANES = 128
KEY = DC + LANES
BLOCKED = -1e30
EXP_SCALE = math.log2(math.e) / math.sqrt(DH + DR)
HEADS_STEP = 8
GROUP = 16
COSTS = {"pack": 5.0, "latent_queries": 0.001, "pass_on": 0.001, "near_rows": 1.0, "early": 3.0, "far_rows": 3.0, "last_rows": 0.001}
VMEM_LIMIT = 20 * 1024 * 1024


def cost(micros):
    return pl.CostEstimate(flops=int(micros * 1e9), bytes_accessed=1024, transcendentals=0)


BF16 = jnp.bfloat16
F32 = jnp.float32

VMEM = pl.BlockSpec(memory_space=pltpu.VMEM)
HBM = pl.BlockSpec(memory_space=pltpu.HBM)
ANYWHERE = pl.BlockSpec(memory_space=pl.ANY)


def iota(shape, dim):
    return lax.broadcasted_iota(jnp.int32, shape, dim)


def span(step, size, first=0):
    return slice(first + step * size, first + (step + 1) * size)


def params():
    return pltpu.CompilerParams(vmem_limit_bytes=VMEM_LIMIT)


def in_vmem(array):
    return pltpu.with_memory_space_constraint(array, pltpu.VMEM)


def dot(a, b):
    return jnp.dot(a, b, preferred_element_type=F32)


def dot_t(a, b):
    return lax.dot_general(a, b, (((1,), (1,)), ((), ())), preferred_element_type=F32)


def in_hbm(array):
    return pltpu.with_memory_space_constraint(array, pltpu.HBM)


def pack_kernel(
    fresh_hbm,
    rope_hbm,
    cached_hbm,
    lat_hbm,
    q_hbm,
    r_hbm,
    length_ref,
    note_ref,
    lat_ref,
    q_ref,
    r_ref,
    rope_buf,
    cached_buf,
    sems,
):
    part = fresh_hbm.shape[0]
    slots = cached_hbm.shape[1]
    me = lax.axis_index("ctx")
    q_first = pl.multiple_of(me * q_ref.shape[1], LANES)
    r_first = pl.multiple_of(me * r_ref.shape[1], LANES)
    pairs = [
        (rope_hbm, rope_buf),
        (cached_hbm, cached_buf),
        (fresh_hbm, note_ref.at[:part, :]),
        (q_hbm.at[0, :, pl.ds(q_first, q_ref.shape[1])], q_ref),
        (r_hbm.at[0, :, pl.ds(r_first, r_ref.shape[1])], r_ref),
        (lat_hbm, lat_ref),
    ]
    copies = [pltpu.make_async_copy(source, target, sems.at[k]) for k, (source, target) in enumerate(pairs)]
    for copy in copies:
        copy.start()
    groups = part // GROUP
    note_ref[part : part + GROUP, :] = jnp.zeros((GROUP, DC), BF16)
    live = jnp.broadcast_to(length_ref[...], (GROUP, LANES)).astype(F32).astype(BF16)
    note_ref[part : part + GROUP, groups * LANES : (groups + 1) * LANES] = live
    copies[0].wait()
    for k in range(groups):
        note_ref[part : part + GROUP, k * LANES : k * LANES + DR] = rope_buf[span(k, GROUP), :]
    copies[1].wait()
    note_ref[part + GROUP :, :slots] = cached_buf[: DR // 2, :]
    note_ref[part + GROUP :, slots:] = cached_buf[DR // 2 :, :]
    for copy in copies[2:]:
        copy.wait()


def pack(fresh, rope, cached_rope, lat, q_nope, q_rope, length, heads):
    part = fresh.shape[0]
    count = q_nope.shape[1]
    return pl.pallas_call(
        pack_kernel,
        out_shape=(
            pltpu.VMEM((part + GROUP + DR // 2, DC), BF16),
            pltpu.VMEM(lat.shape, BF16),
            pltpu.VMEM((count, heads * DH), BF16),
            pltpu.VMEM((count, heads * DR), BF16),
        ),
        in_specs=[HBM] * 6 + [VMEM],
        out_specs=(VMEM, VMEM, VMEM, VMEM),
        scratch_shapes=[
            pltpu.VMEM(rope.shape, BF16),
            pltpu.VMEM(cached_rope.shape, BF16),
            pltpu.SemaphoreType.DMA((6,)),
        ],
        compiler_params=params(),
        cost_estimate=cost(COSTS["pack"]),
        name="pack",
    )(*[in_hbm(array) for array in (fresh, rope, cached_rope, lat, q_nope, q_rope)], length)


def queries_kernel(q_ref, r_ref, w_ref, out_ref):
    count = q_ref.shape[0]
    heads = out_ref.shape[0] // count
    lane = iota((count, LANES), 1)
    side = jnp.where(lane == DR, 1.0, 0.0)
    for pair in range(heads // 2):
        both = r_ref[:, span(pair, LANES)].astype(F32)
        for odd in range(2):
            head = 2 * pair + odd
            one = pltpu.roll(both, DR, 1) if odd else both
            out_ref[span(head, count), :DC] = dot_t(q_ref[:, span(head, DH)], w_ref[:, span(head, DH)]).astype(BF16)
            out_ref[span(head, count), DC:] = jnp.where(lane < DR, one, side).astype(BF16)


def make_queries(q, r, w_key):
    count = q.shape[0]
    heads = w_key.shape[1] // DH
    return pl.pallas_call(
        queries_kernel,
        out_shape=pltpu.VMEM((heads * count, KEY), BF16),
        in_specs=[VMEM] * 3,
        out_specs=VMEM,
        compiler_params=params(),
        cost_estimate=cost(COSTS["latent_queries"]),
        name="latent_queries",
    )(q, r, in_vmem(w_key))


def pass_kernel(array_ref, token_ref, out_ref):
    out_ref[...] = array_ref[...]


def after(array, token):
    return pl.pallas_call(
        pass_kernel,
        out_shape=pltpu.VMEM(array.shape, BF16),
        in_specs=[VMEM, ANYWHERE],
        out_specs=VMEM,
        compiler_params=params(),
        cost_estimate=cost(COSTS["pass_on"]),
        name="pass_on",
    )(array, token)


def put_cached(key_buf, first, lat_ref, note_ref):
    slots = lat_ref.shape[0]
    key_buf[first : first + slots, :DC] = lat_ref[...]
    key_buf[first : first + slots, DC:] = masked_rope(note_ref, slots)


def masked_rope(note_ref, slots):
    part = note_ref.shape[0] - GROUP - DR // 2
    lane = part // GROUP * LANES
    live = note_ref[part : part + 1, lane : lane + 1].astype(F32)
    blocked = jnp.where(iota((LANES - DR, slots), 1).astype(F32) < live, 0.0, BLOCKED)
    blocked = jnp.where(iota((LANES - DR, slots), 0) == 0, blocked, 0.0)
    rope = note_ref[part + GROUP :, :].astype(F32)
    return jnp.concatenate([rope[:, :slots], rope[:, slots:], blocked], axis=0).T.astype(BF16)


def put_fresh(key_buf, first, note_refs):
    part = note_refs[0].shape[0] - GROUP - DR // 2
    for index, note_ref in enumerate(note_refs):
        key_buf[first + index * part : first + (index + 1) * part, :DC] = note_ref[:part, :]
        for k in range(part // GROUP):
            rows = span(k, GROUP, first + index * part)
            key_buf[rows, DC:] = note_ref[part : part + GROUP, k * LANES : (k + 1) * LANES]


def causal(part, blocks):
    count = part * blocks
    me = lax.axis_index("ctx")
    col = iota((count, count), 1)
    origin = jnp.bitwise_xor(jnp.full((count, count), me, jnp.int32), col // part)
    return jnp.where(origin * part + col % part <= iota((count, count), 0), 0.0, BLOCKED)


def pipeline(steps, scores, weigh, collect):
    upcoming, previous = scores(0), None
    for step in range(steps):
        now = upcoming
        if step + 1 < steps:
            upcoming = scores(step + 1)
        if previous is not None:
            collect(step - 1, *previous)
        previous = weigh(step, now)
    collect(steps - 1, *previous)


def exponents(s, level, total):
    parts = []
    for k in range(s.shape[1] // LANES):
        p = jnp.exp2((s[:, k * LANES : (k + 1) * LANES] - level) * EXP_SCALE)
        total = p if total is None else total + p
        parts.append(p.astype(BF16))
    return jnp.concatenate(parts, axis=1), total


def state_shapes(rows):
    return (pltpu.VMEM((rows, DV), F32), pltpu.VMEM((rows, LANES), F32), pltpu.VMEM((rows, LANES), F32))


def near_kernel(q_ref, *refs, cached, size):
    w_hbm, out_ref, sum_ref, max_ref, w_ref, key_buf, sem = refs[2 * cached :]
    copy = pltpu.make_async_copy(w_hbm, w_ref, sem)
    copy.start()
    slots = refs[0].shape[0]
    for k in range(cached):
        put_cached(key_buf, k * slots, refs[2 * k], refs[2 * k + 1])
    count = size // HEADS_STEP

    def scores(step):
        return dot_t(q_ref[span(step, size), :], key_buf[...])

    def weigh(step, s):
        level = jnp.max(s, axis=1, keepdims=True)
        p, total = exponents(s, level, None)
        sum_ref[span(step, size), :] = total
        max_ref[span(step, size), :] = jnp.broadcast_to(level, (size, LANES))
        return (p,)

    def collect(step, p):
        mixed = dot(p, key_buf[:, :DC]).astype(BF16)
        if step == 0:
            copy.wait()
        for k in range(HEADS_STEP):
            head = step * HEADS_STEP + k
            out_ref[span(head, count), :] = dot(mixed[span(k, count), :], w_ref[:, span(head, DV)])

    pipeline(q_ref.shape[0] // size, scores, weigh, collect)


def near_pass(q, blocks, w_value, count):
    rows = q.shape[0]
    keys = sum(block[0].shape[0] for block in blocks)
    return pl.pallas_call(
        functools.partial(near_kernel, cached=len(blocks), size=HEADS_STEP * count),
        out_shape=(*state_shapes(rows), pltpu.VMEM(w_value.shape, BF16)),
        in_specs=[VMEM] * (1 + 2 * len(blocks)) + [HBM],
        out_specs=(VMEM, VMEM, VMEM, VMEM),
        scratch_shapes=[pltpu.VMEM((keys, KEY), BF16), pltpu.SemaphoreType.DMA],
        compiler_params=params(),
        cost_estimate=cost(COSTS["near_rows"]),
        name="near_rows",
    )(q, *[array for block in blocks for array in block], in_hbm(w_value))


def early_kernel(q_ref, lat_ref, w_ref, out_ref, value_ref, *, size):
    for step in range(q_ref.shape[0] // size):
        rows = span(step, size)
        out_ref[rows, :] = dot_t(q_ref[rows, :DC], lat_ref[...])
        cols = span(step, HEADS_STEP * DV)
        value_ref[:, cols] = dot(lat_ref[...], w_ref[:, cols]).astype(BF16)


def early_pass(q, lat, w_value, count):
    rows = q.shape[0]
    slots = lat.shape[0]
    return pl.pallas_call(
        functools.partial(early_kernel, size=HEADS_STEP * count),
        out_shape=(pltpu.VMEM((rows, slots), F32), pltpu.VMEM((slots, w_value.shape[1]), BF16)),
        in_specs=[VMEM] * 3,
        out_specs=(VMEM, VMEM),
        compiler_params=params(),
        cost_estimate=cost(COSTS["early"]),
        name="early",
    )(q, lat, w_value)


def far_kernel(
    q_ref,
    note_ref,
    s_ref,
    value_ref,
    out_in,
    sum_in,
    max_in,
    lat_ref,
    w_ref,
    out_ref,
    sum_ref,
    max_ref,
    next_ref,
    ext_buf,
    *,
    size,
):
    ext_buf[...] = masked_rope(note_ref, value_ref.shape[0])
    count = size // HEADS_STEP

    def scores(step):
        rows = span(step, size)
        return s_ref[rows, :] + dot_t(q_ref[rows, DC:], ext_buf[...])

    def weigh(step, s):
        rows = span(step, size)
        before = max_in[rows, :]
        level = jnp.maximum(before, jnp.max(s, axis=1, keepdims=True))
        factor = jnp.exp2((before - level) * EXP_SCALE)
        p, total = exponents(s, level, sum_in[rows, :] * factor)
        sum_ref[rows, :] = total
        max_ref[rows, :] = level
        return p, factor

    def collect(step, p, factor):
        cols = span(step, HEADS_STEP * DV)
        next_ref[:, cols] = dot(lat_ref[...], w_ref[:, cols]).astype(BF16)
        for k in range(HEADS_STEP):
            head = step * HEADS_STEP + k
            grown = dot(p[span(k, count), :], value_ref[:, span(head, DV)])
            out_ref[span(head, count), :] = out_in[span(head, count), :] * factor[span(k, count), :] + grown

    pipeline(q_ref.shape[0] // size, scores, weigh, collect)


def far_pass(q, note, scores, values, state, next_lat, w_value, count):
    rows = q.shape[0]
    return pl.pallas_call(
        functools.partial(far_kernel, size=HEADS_STEP * count),
        out_shape=(*state_shapes(rows), pltpu.VMEM((next_lat.shape[0], w_value.shape[1]), BF16)),
        in_specs=[VMEM] * 9,
        out_specs=(VMEM, VMEM, VMEM, VMEM),
        scratch_shapes=[pltpu.VMEM((values.shape[0], LANES), BF16)],
        compiler_params=params(),
        cost_estimate=cost(COSTS["far_rows"]),
        name="far_rows",
    )(q, note, scores, values, *state, next_lat, w_value)


def last_kernel(q_ref, lat_ref, value_ref, *refs, blocks, size):
    notes, refs = refs[:blocks], refs[blocks:]
    out_in, sum_in, max_in, w_ref, out_hbm, key_buf, out_buf, sems = refs
    slots = lat_ref.shape[0]
    count = out_hbm.shape[0]
    put_cached(key_buf, 0, lat_ref, notes[-1])
    put_fresh(key_buf, slots, notes)
    bias = jnp.concatenate([causal(count // blocks, blocks)] * HEADS_STEP, axis=0)
    copies = []

    def scores(step):
        s = dot_t(q_ref[span(step, size), :], key_buf[...])
        return jnp.concatenate([s[:, :slots], s[:, slots:] + bias], axis=1)

    def weigh(step, s):
        rows = span(step, size)
        before = max_in[rows, :]
        level = jnp.maximum(before, jnp.max(s, axis=1, keepdims=True))
        factor = jnp.exp2((before - level) * EXP_SCALE)
        p, total = exponents(s, level, sum_in[rows, :] * factor)
        inverse = 1.0 / jnp.sum(total, axis=1, keepdims=True)
        return p, factor * inverse, inverse

    def collect(step, p, factor, inverse):
        fresh = dot(key_buf[slots:, :DC], w_ref[:, span(step, HEADS_STEP * DV)]).astype(BF16)
        for k in range(HEADS_STEP):
            head = step * HEADS_STEP + k
            part = span(k, count)
            grown = dot(p[part, :slots], value_ref[:, span(head, DV)]) + dot(p[part, slots:], fresh[:, span(k, DV)])
            whole = out_in[span(head, count), :] * factor[part, :] + grown * inverse[part, :]
            out_buf[:, span(head, DV)] = whole.astype(BF16)
        cols = span(step, HEADS_STEP * DV)
        copies.append(pltpu.make_async_copy(out_buf.at[:, cols], out_hbm.at[:, cols], sems.at[step]))
        copies[-1].start()

    pipeline(q_ref.shape[0] // size, scores, weigh, collect)
    for copy in copies:
        copy.wait()


def last_pass(q, lat, values, notes, state, w_value, count):
    rows = q.shape[0]
    shape = (count, w_value.shape[1])
    return pl.pallas_call(
        functools.partial(last_kernel, blocks=len(notes), size=HEADS_STEP * count),
        out_shape=jax.ShapeDtypeStruct(shape, BF16),
        in_specs=[VMEM] * (7 + len(notes)),
        out_specs=HBM,
        scratch_shapes=[
            pltpu.VMEM((lat.shape[0] + count, KEY), BF16),
            pltpu.VMEM(shape, BF16),
            pltpu.SemaphoreType.DMA((rows // (HEADS_STEP * count),)),
        ],
        compiler_params=params(),
        cost_estimate=cost(COSTS["last_rows"]),
        name="last_rows",
    )(q, lat, values, *notes, *state, w_value)


def hop(array, bit):
    size = lax.axis_size("ctx")
    return lax.ppermute(array, "ctx", [(k, k ^ bit) for k in range(size)])


def shards(q_nope, q_rope, cache_latent, cache_rope, new_latent, new_rope, lengths, w_key, w_value):
    count = q_nope.shape[1]
    lat = cache_latent[0]
    far_lat, near_lat = hop(lat, 2), hop(lat, 1)
    heads = w_key.shape[1] // DH
    note, lat, own_q, own_r = pack(
        new_latent[0], new_rope[0], cache_rope[0].T, lat, q_nope, q_rope, lengths, heads
    )
    near_note = hop(note, 1)
    q = make_queries(own_q, own_r, w_key)
    far_note = hop(after(note, q), 2)
    *state, w_value = near_pass(q, [(lat, note), (near_lat, near_note)], w_value, count)
    last_lat = hop(after(far_lat, state[2]), 1)
    scores, values = early_pass(q, far_lat, w_value, count)
    last_note = hop(after(far_note, scores), 1)
    *state, values = far_pass(q, far_note, scores, values, state, last_lat, w_value, count)
    notes = [note, near_note, far_note, last_note]
    return last_pass(q, last_lat, values, notes, state, w_value, count)[None]


def solution(mesh):
    return jax.shard_map(
        shards,
        mesh=mesh,
        in_specs=(
            P("req", None, None),
            P("req", None, None),
            P("req", "ctx", None),
            P("req", "ctx", None),
            P("req", "ctx", None),
            P("req", "ctx", None),
            P("req", "ctx"),
            P(None, "ctx"),
            P(None, "ctx"),
        ),
        out_specs=P("req", None, "ctx"),
        check_vma=False,
    )
```

```python
import functools
import math

import jax
import jax.numpy as jnp
from jax import lax
from jax.experimental import pallas as pl
from jax.experimental.pallas import tpu as pltpu
from jax.sharding import PartitionSpec as P

DC = 512
DR = 64
DH = 128
DV = 128
LANES = 128
KEY = DC + LANES
BLOCKED = -1e30
EXP_SCALE = math.log2(math.e) / math.sqrt(DH + DR)
HEADS_STEP = 4
GROUP = 16
COSTS = {"pack": 0.6, "latent_queries": 0.001, "pass_on": 0.001, "near_rows": 1.0, "early": 3.0, "far_rows": 3.0, "last_rows": 0.001}
VMEM_LIMIT = 20 * 1024 * 1024


def cost(micros):
    return pl.CostEstimate(flops=int(micros * 1e9), bytes_accessed=1024, transcendentals=0)


BF16 = jnp.bfloat16
F32 = jnp.float32

VMEM = pl.BlockSpec(memory_space=pltpu.VMEM)
HBM = pl.BlockSpec(memory_space=pltpu.HBM)
ANYWHERE = pl.BlockSpec(memory_space=pl.ANY)


def iota(shape, dim):
    return lax.broadcasted_iota(jnp.int32, shape, dim)


def span(step, size, first=0):
    return slice(first + step * size, first + (step + 1) * size)


def params():
    return pltpu.CompilerParams(vmem_limit_bytes=VMEM_LIMIT)


def in_vmem(array):
    return pltpu.with_memory_space_constraint(array, pltpu.VMEM)


def dot(a, b):
    return jnp.dot(a, b, preferred_element_type=F32)


def dot_t(a, b):
    return lax.dot_general(a, b, (((1,), (1,)), ((), ())), preferred_element_type=F32)


def in_hbm(array):
    return pltpu.with_memory_space_constraint(array, pltpu.HBM)


def pack_kernel(
    fresh_hbm,
    rope_hbm,
    cached_hbm,
    lat_hbm,
    q_hbm,
    r_hbm,
    length_ref,
    note_ref,
    lat_ref,
    q_ref,
    r_ref,
    rope_buf,
    cached_buf,
    sems,
):
    part = fresh_hbm.shape[0]
    slots = cached_hbm.shape[1]
    me = lax.axis_index("ctx")
    q_first = pl.multiple_of(me * q_ref.shape[1], LANES)
    r_first = pl.multiple_of(me * r_ref.shape[1], LANES)
    pairs = [
        (rope_hbm, rope_buf),
        (cached_hbm, cached_buf),
        (fresh_hbm, note_ref.at[:part, :]),
        (q_hbm.at[0, :, pl.ds(q_first, q_ref.shape[1])], q_ref),
        (r_hbm.at[0, :, pl.ds(r_first, r_ref.shape[1])], r_ref),
        (lat_hbm, lat_ref),
    ]
    copies = [pltpu.make_async_copy(source, target, sems.at[k]) for k, (source, target) in enumerate(pairs)]
    for copy in copies:
        copy.start()
    groups = part // GROUP
    note_ref[part : part + GROUP, :] = jnp.zeros((GROUP, DC), BF16)
    live = jnp.broadcast_to(length_ref[...], (GROUP, LANES)).astype(F32).astype(BF16)
    note_ref[part : part + GROUP, groups * LANES : (groups + 1) * LANES] = live
    copies[0].wait()
    for k in range(groups):
        note_ref[part : part + GROUP, k * LANES : k * LANES + DR] = rope_buf[span(k, GROUP), :]
    copies[1].wait()
    note_ref[part + GROUP :, :slots] = cached_buf[: DR // 2, :]
    note_ref[part + GROUP :, slots:] = cached_buf[DR // 2 :, :]
    for copy in copies[2:]:
        copy.wait()


def pack(fresh, rope, cached_rope, lat, q_nope, q_rope, length, heads):
    part = fresh.shape[0]
    count = q_nope.shape[1]
    return pl.pallas_call(
        pack_kernel,
        out_shape=(
            pltpu.VMEM((part + GROUP + DR // 2, DC), BF16),
            pltpu.VMEM(lat.shape, BF16),
            pltpu.VMEM((count, heads * DH), BF16),
            pltpu.VMEM((count, heads * DR), BF16),
        ),
        in_specs=[HBM] * 6 + [VMEM],
        out_specs=(VMEM, VMEM, VMEM, VMEM),
        scratch_shapes=[
            pltpu.VMEM(rope.shape, BF16),
            pltpu.VMEM(cached_rope.shape, BF16),
            pltpu.SemaphoreType.DMA((6,)),
        ],
        compiler_params=params(),
        cost_estimate=cost(COSTS["pack"]),
        name="pack",
    )(*[in_hbm(array) for array in (fresh, rope, cached_rope, lat, q_nope, q_rope)], length)


def queries_kernel(q_ref, r_ref, w_ref, out_ref):
    count = q_ref.shape[0]
    heads = out_ref.shape[0] // count
    lane = iota((count, LANES), 1)
    side = jnp.where(lane == DR, 1.0, 0.0)
    for pair in range(heads // 2):
        both = r_ref[:, span(pair, LANES)].astype(F32)
        for odd in range(2):
            head = 2 * pair + odd
            one = pltpu.roll(both, DR, 1) if odd else both
            out_ref[span(head, count), :DC] = dot_t(q_ref[:, span(head, DH)], w_ref[:, span(head, DH)]).astype(BF16)
            out_ref[span(head, count), DC:] = jnp.where(lane < DR, one, side).astype(BF16)


def make_queries(q, r, w_key):
    count = q.shape[0]
    heads = w_key.shape[1] // DH
    return pl.pallas_call(
        queries_kernel,
        out_shape=pltpu.VMEM((heads * count, KEY), BF16),
        in_specs=[VMEM] * 3,
        out_specs=VMEM,
        compiler_params=params(),
        cost_estimate=cost(COSTS["latent_queries"]),
        name="latent_queries",
    )(q, r, in_vmem(w_key))


def pass_kernel(array_ref, token_ref, out_ref):
    out_ref[...] = array_ref[...]


def after(array, token):
    return pl.pallas_call(
        pass_kernel,
        out_shape=pltpu.VMEM(array.shape, BF16),
        in_specs=[VMEM, ANYWHERE],
        out_specs=VMEM,
        compiler_params=params(),
        cost_estimate=cost(COSTS["pass_on"]),
        name="pass_on",
    )(array, token)


def put_cached(key_buf, first, lat_ref, note_ref):
    slots = lat_ref.shape[0]
    key_buf[first : first + slots, :DC] = lat_ref[...]
    key_buf[first : first + slots, DC:] = masked_rope(note_ref, slots)


def masked_rope(note_ref, slots):
    part = note_ref.shape[0] - GROUP - DR // 2
    lane = part // GROUP * LANES
    live = note_ref[part : part + 1, lane : lane + 1].astype(F32)
    blocked = jnp.where(iota((LANES - DR, slots), 1).astype(F32) < live, 0.0, BLOCKED)
    blocked = jnp.where(iota((LANES - DR, slots), 0) == 0, blocked, 0.0)
    rope = note_ref[part + GROUP :, :].astype(F32)
    return jnp.concatenate([rope[:, :slots], rope[:, slots:], blocked], axis=0).T.astype(BF16)


def put_fresh(key_buf, first, note_refs):
    part = note_refs[0].shape[0] - GROUP - DR // 2
    for index, note_ref in enumerate(note_refs):
        key_buf[first + index * part : first + (index + 1) * part, :DC] = note_ref[:part, :]
        for k in range(part // GROUP):
            rows = span(k, GROUP, first + index * part)
            key_buf[rows, DC:] = note_ref[part : part + GROUP, k * LANES : (k + 1) * LANES]


def causal(part, blocks):
    count = part * blocks
    me = lax.axis_index("ctx")
    col = iota((count, count), 1)
    origin = jnp.bitwise_xor(jnp.full((count, count), me, jnp.int32), col // part)
    return jnp.where(origin * part + col % part <= iota((count, count), 0), 0.0, BLOCKED)


def pipeline(steps, scores, weigh, collect):
    upcoming, previous = scores(0), None
    for step in range(steps):
        now = upcoming
        if step + 1 < steps:
            upcoming = scores(step + 1)
        if previous is not None:
            collect(step - 1, *previous)
        previous = weigh(step, now)
    collect(steps - 1, *previous)


def exponents(s, level, total):
    parts = []
    for k in range(s.shape[1] // LANES):
        p = jnp.exp2((s[:, k * LANES : (k + 1) * LANES] - level) * EXP_SCALE)
        total = p if total is None else total + p
        parts.append(p.astype(BF16))
    return jnp.concatenate(parts, axis=1), total


def state_shapes(rows):
    return (pltpu.VMEM((rows, DV), F32), pltpu.VMEM((rows, LANES), F32), pltpu.VMEM((rows, LANES), F32))


def near_kernel(q_ref, *refs, cached, size):
    w_hbm, out_ref, sum_ref, max_ref, w_ref, key_buf, sem = refs[2 * cached :]
    copy = pltpu.make_async_copy(w_hbm, w_ref, sem)
    copy.start()
    slots = refs[0].shape[0]
    for k in range(cached):
        put_cached(key_buf, k * slots, refs[2 * k], refs[2 * k + 1])
    count = size // HEADS_STEP

    def scores(step):
        return dot_t(q_ref[span(step, size), :], key_buf[...])

    def weigh(step, s):
        level = jnp.max(s, axis=1, keepdims=True)
        p, total = exponents(s, level, None)
        sum_ref[span(step, size), :] = total
        max_ref[span(step, size), :] = jnp.broadcast_to(level, (size, LANES))
        return (p,)

    def collect(step, p):
        mixed = dot(p, key_buf[:, :DC]).astype(BF16)
        if step == 0:
            copy.wait()
        for k in range(HEADS_STEP):
            head = step * HEADS_STEP + k
            out_ref[span(head, count), :] = dot(mixed[span(k, count), :], w_ref[:, span(head, DV)])

    pipeline(q_ref.shape[0] // size, scores, weigh, collect)


def near_pass(q, blocks, w_value, count):
    rows = q.shape[0]
    keys = sum(block[0].shape[0] for block in blocks)
    return pl.pallas_call(
        functools.partial(near_kernel, cached=len(blocks), size=HEADS_STEP * count),
        out_shape=(*state_shapes(rows), pltpu.VMEM(w_value.shape, BF16)),
        in_specs=[VMEM] * (1 + 2 * len(blocks)) + [HBM],
        out_specs=(VMEM, VMEM, VMEM, VMEM),
        scratch_shapes=[pltpu.VMEM((keys, KEY), BF16), pltpu.SemaphoreType.DMA],
        compiler_params=params(),
        cost_estimate=cost(COSTS["near_rows"]),
        name="near_rows",
    )(q, *[array for block in blocks for array in block], in_hbm(w_value))


def early_kernel(q_ref, lat_ref, w_ref, out_ref, value_ref, *, size):
    for step in range(q_ref.shape[0] // size):
        rows = span(step, size)
        out_ref[rows, :] = dot_t(q_ref[rows, :DC], lat_ref[...])
        cols = span(step, HEADS_STEP * DV)
        value_ref[:, cols] = dot(lat_ref[...], w_ref[:, cols]).astype(BF16)


def early_pass(q, lat, w_value, count):
    rows = q.shape[0]
    slots = lat.shape[0]
    return pl.pallas_call(
        functools.partial(early_kernel, size=HEADS_STEP * count),
        out_shape=(pltpu.VMEM((rows, slots), F32), pltpu.VMEM((slots, w_value.shape[1]), BF16)),
        in_specs=[VMEM] * 3,
        out_specs=(VMEM, VMEM),
        compiler_params=params(),
        cost_estimate=cost(COSTS["early"]),
        name="early",
    )(q, lat, w_value)


def far_kernel(
    q_ref,
    note_ref,
    s_ref,
    value_ref,
    out_in,
    sum_in,
    max_in,
    lat_ref,
    w_ref,
    out_ref,
    sum_ref,
    max_ref,
    next_ref,
    ext_buf,
    *,
    size,
):
    ext_buf[...] = masked_rope(note_ref, value_ref.shape[0])
    count = size // HEADS_STEP

    def scores(step):
        rows = span(step, size)
        return s_ref[rows, :] + dot_t(q_ref[rows, DC:], ext_buf[...])

    def weigh(step, s):
        rows = span(step, size)
        before = max_in[rows, :]
        level = jnp.maximum(before, jnp.max(s, axis=1, keepdims=True))
        factor = jnp.exp2((before - level) * EXP_SCALE)
        p, total = exponents(s, level, sum_in[rows, :] * factor)
        sum_ref[rows, :] = total
        max_ref[rows, :] = level
        cols = span(step, HEADS_STEP * DV)
        next_ref[:, cols] = dot(lat_ref[...], w_ref[:, cols]).astype(BF16)
        return p, factor

    def collect(step, p, factor):
        for k in range(HEADS_STEP):
            head = step * HEADS_STEP + k
            grown = dot(p[span(k, count), :], value_ref[:, span(head, DV)])
            out_ref[span(head, count), :] = out_in[span(head, count), :] * factor[span(k, count), :] + grown

    pipeline(q_ref.shape[0] // size, scores, weigh, collect)


def far_pass(q, note, scores, values, state, next_lat, w_value, count):
    rows = q.shape[0]
    return pl.pallas_call(
        functools.partial(far_kernel, size=HEADS_STEP * count),
        out_shape=(*state_shapes(rows), pltpu.VMEM((next_lat.shape[0], w_value.shape[1]), BF16)),
        in_specs=[VMEM] * 9,
        out_specs=(VMEM, VMEM, VMEM, VMEM),
        scratch_shapes=[pltpu.VMEM((values.shape[0], LANES), BF16)],
        compiler_params=params(),
        cost_estimate=cost(COSTS["far_rows"]),
        name="far_rows",
    )(q, note, scores, values, *state, next_lat, w_value)


def last_kernel(q_ref, lat_ref, value_ref, *refs, blocks, size):
    notes, refs = refs[:blocks], refs[blocks:]
    out_in, sum_in, max_in, w_ref, out_hbm, key_buf, out_buf, sems = refs
    slots = lat_ref.shape[0]
    count = out_hbm.shape[0]
    put_cached(key_buf, 0, lat_ref, notes[-1])
    put_fresh(key_buf, slots, notes)
    bias = jnp.concatenate([causal(count // blocks, blocks)] * HEADS_STEP, axis=0)
    copies = []

    def scores(step):
        s = dot_t(q_ref[span(step, size), :], key_buf[...])
        return jnp.concatenate([s[:, :slots], s[:, slots:] + bias], axis=1)

    def weigh(step, s):
        rows = span(step, size)
        before = max_in[rows, :]
        level = jnp.maximum(before, jnp.max(s, axis=1, keepdims=True))
        factor = jnp.exp2((before - level) * EXP_SCALE)
        p, total = exponents(s, level, sum_in[rows, :] * factor)
        inverse = 1.0 / jnp.sum(total, axis=1, keepdims=True)
        fresh = dot(key_buf[slots:, :DC], w_ref[:, span(step, HEADS_STEP * DV)]).astype(BF16)
        return p, factor * inverse, inverse, fresh

    def collect(step, p, factor, inverse, fresh):
        for k in range(HEADS_STEP):
            head = step * HEADS_STEP + k
            part = span(k, count)
            grown = dot(p[part, :slots], value_ref[:, span(head, DV)]) + dot(p[part, slots:], fresh[:, span(k, DV)])
            whole = out_in[span(head, count), :] * factor[part, :] + grown * inverse[part, :]
            out_buf[:, span(head, DV)] = whole.astype(BF16)
        cols = span(step, HEADS_STEP * DV)
        copies.append(pltpu.make_async_copy(out_buf.at[:, cols], out_hbm.at[:, cols], sems.at[step]))
        copies[-1].start()

    pipeline(q_ref.shape[0] // size, scores, weigh, collect)
    for copy in copies:
        copy.wait()


def last_pass(q, lat, values, notes, state, w_value, count):
    rows = q.shape[0]
    shape = (count, w_value.shape[1])
    return pl.pallas_call(
        functools.partial(last_kernel, blocks=len(notes), size=HEADS_STEP * count),
        out_shape=jax.ShapeDtypeStruct(shape, BF16),
        in_specs=[VMEM] * (7 + len(notes)),
        out_specs=HBM,
        scratch_shapes=[
            pltpu.VMEM((lat.shape[0] + count, KEY), BF16),
            pltpu.VMEM(shape, BF16),
            pltpu.SemaphoreType.DMA((rows // (HEADS_STEP * count),)),
        ],
        compiler_params=params(),
        cost_estimate=cost(COSTS["last_rows"]),
        name="last_rows",
    )(q, lat, values, *notes, *state, w_value)


def hop(array, bit):
    size = lax.axis_size("ctx")
    return lax.ppermute(array, "ctx", [(k, k ^ bit) for k in range(size)])


def shards(q_nope, q_rope, cache_latent, cache_rope, new_latent, new_rope, lengths, w_key, w_value):
    count = q_nope.shape[1]
    lat = cache_latent[0]
    far_lat, near_lat = hop(lat, 2), hop(lat, 1)
    heads = w_key.shape[1] // DH
    note, lat, own_q, own_r = pack(
        new_latent[0], new_rope[0], cache_rope[0].T, lat, q_nope, q_rope, lengths, heads
    )
    near_note = hop(note, 1)
    q = make_queries(own_q, own_r, w_key)
    far_note = hop(after(note, q), 2)
    *state, w_value = near_pass(q, [(lat, note), (near_lat, near_note)], w_value, count)
    last_lat = hop(after(far_lat, state[2]), 1)
    scores, values = early_pass(q, far_lat, w_value, count)
    last_note = hop(after(far_note, scores), 1)
    *state, values = far_pass(q, far_note, scores, values, state, last_lat, w_value, count)
    notes = [note, near_note, far_note, last_note]
    return last_pass(q, last_lat, values, notes, state, w_value, count)[None]


def solution(mesh):
    return jax.shard_map(
        shards,
        mesh=mesh,
        in_specs=(
            P("req", None, None),
            P("req", None, None),
            P("req", "ctx", None),
            P("req", "ctx", None),
            P("req", "ctx", None),
            P("req", "ctx", None),
            P("req", "ctx"),
            P(None, "ctx"),
            P(None, "ctx"),
        ),
        out_specs=P("req", None, "ctx"),
        check_vma=False,
    )
```

```python
import functools
import math

import jax
import jax.numpy as jnp
from jax import lax
from jax.experimental import pallas as pl
from jax.experimental.pallas import tpu as pltpu
from jax.sharding import PartitionSpec as P

DC = 512
DR = 64
DH = 128
DV = 128
LANES = 128
KEY = DC + LANES
BLOCKED = -1e30
EXP_SCALE = math.log2(math.e) / math.sqrt(DH + DR)
HEADS_STEP = 4
GROUP = 16
COSTS = {"pack": 0.6, "latent_queries": 0.001, "pass_on": 0.001, "near_rows": 1.0, "early": 3.0, "far_rows": 3.0, "last_rows": 0.001}
VMEM_LIMIT = 20 * 1024 * 1024


def cost(micros):
    return pl.CostEstimate(flops=int(micros * 1e9), bytes_accessed=1024, transcendentals=0)


BF16 = jnp.bfloat16
F32 = jnp.float32

VMEM = pl.BlockSpec(memory_space=pltpu.VMEM)
HBM = pl.BlockSpec(memory_space=pltpu.HBM)
ANYWHERE = pl.BlockSpec(memory_space=pl.ANY)


def iota(shape, dim):
    return lax.broadcasted_iota(jnp.int32, shape, dim)


def span(step, size, first=0):
    return slice(first + step * size, first + (step + 1) * size)


def params():
    return pltpu.CompilerParams(vmem_limit_bytes=VMEM_LIMIT)


def in_vmem(array):
    return pltpu.with_memory_space_constraint(array, pltpu.VMEM)


def dot(a, b):
    return jnp.dot(a, b, preferred_element_type=F32)


def dot_t(a, b):
    return lax.dot_general(a, b, (((1,), (1,)), ((), ())), preferred_element_type=F32)


def in_hbm(array):
    return pltpu.with_memory_space_constraint(array, pltpu.HBM)


def pack_kernel(
    fresh_hbm,
    rope_hbm,
    cached_hbm,
    lat_hbm,
    q_hbm,
    r_hbm,
    length_ref,
    note_ref,
    lat_ref,
    q_ref,
    r_ref,
    rope_buf,
    cached_buf,
    sems,
):
    part = fresh_hbm.shape[0]
    slots = cached_hbm.shape[1]
    me = lax.axis_index("ctx")
    q_first = pl.multiple_of(me * q_ref.shape[1], LANES)
    r_first = pl.multiple_of(me * r_ref.shape[1], LANES)
    pairs = [
        (rope_hbm, rope_buf),
        (cached_hbm, cached_buf),
        (fresh_hbm, note_ref.at[:part, :]),
        (q_hbm.at[0, :, pl.ds(q_first, q_ref.shape[1])], q_ref),
        (r_hbm.at[0, :, pl.ds(r_first, r_ref.shape[1])], r_ref),
        (lat_hbm, lat_ref),
    ]
    copies = [pltpu.make_async_copy(source, target, sems.at[k]) for k, (source, target) in enumerate(pairs)]
    for copy in copies:
        copy.start()
    groups = part // GROUP
    note_ref[part : part + GROUP, :] = jnp.zeros((GROUP, DC), BF16)
    live = jnp.broadcast_to(length_ref[...], (GROUP, LANES)).astype(F32).astype(BF16)
    note_ref[part : part + GROUP, groups * LANES : (groups + 1) * LANES] = live
    copies[0].wait()
    for k in range(groups):
        note_ref[part : part + GROUP, k * LANES : k * LANES + DR] = rope_buf[span(k, GROUP), :]
    copies[1].wait()
    note_ref[part + GROUP :, :slots] = cached_buf[: DR // 2, :]
    note_ref[part + GROUP :, slots:] = cached_buf[DR // 2 :, :]
    for copy in copies[2:]:
        copy.wait()


def pack(fresh, rope, cached_rope, lat, q_nope, q_rope, length, heads):
    part = fresh.shape[0]
    count = q_nope.shape[1]
    return pl.pallas_call(
        pack_kernel,
        out_shape=(
            pltpu.VMEM((part + GROUP + DR // 2, DC), BF16),
            pltpu.VMEM(lat.shape, BF16),
            pltpu.VMEM((count, heads * DH), BF16),
            pltpu.VMEM((count, heads * DR), BF16),
        ),
        in_specs=[HBM] * 6 + [VMEM],
        out_specs=(VMEM, VMEM, VMEM, VMEM),
        scratch_shapes=[
            pltpu.VMEM(rope.shape, BF16),
            pltpu.VMEM(cached_rope.shape, BF16),
            pltpu.SemaphoreType.DMA((6,)),
        ],
        compiler_params=params(),
        cost_estimate=cost(COSTS["pack"]),
        name="pack",
    )(*[in_hbm(array) for array in (fresh, rope, cached_rope, lat, q_nope, q_rope)], length)


def queries_kernel(q_ref, r_ref, w_ref, out_ref):
    count = q_ref.shape[0]
    heads = out_ref.shape[0] // count
    lane = iota((count, LANES), 1)
    side = jnp.where(lane == DR, 1.0, 0.0)
    for pair in range(heads // 2):
        both = r_ref[:, span(pair, LANES)].astype(F32)
        for odd in range(2):
            head = 2 * pair + odd
            one = pltpu.roll(both, DR, 1) if odd else both
            out_ref[span(head, count), :DC] = dot_t(q_ref[:, span(head, DH)], w_ref[:, span(head, DH)]).astype(BF16)
            out_ref[span(head, count), DC:] = jnp.where(lane < DR, one, side).astype(BF16)


def make_queries(q, r, w_key):
    count = q.shape[0]
    heads = w_key.shape[1] // DH
    return pl.pallas_call(
        queries_kernel,
        out_shape=pltpu.VMEM((heads * count, KEY), BF16),
        in_specs=[VMEM] * 3,
        out_specs=VMEM,
        compiler_params=params(),
        cost_estimate=cost(COSTS["latent_queries"]),
        name="latent_queries",
    )(q, r, in_vmem(w_key))


def pass_kernel(array_ref, token_ref, out_ref):
    out_ref[...] = array_ref[...]


def after(array, token):
    return pl.pallas_call(
        pass_kernel,
        out_shape=pltpu.VMEM(array.shape, BF16),
        in_specs=[VMEM, ANYWHERE],
        out_specs=VMEM,
        compiler_params=params(),
        cost_estimate=cost(COSTS["pass_on"]),
        name="pass_on",
    )(array, token)


def put_cached(key_buf, first, lat_ref, note_ref):
    slots = lat_ref.shape[0]
    key_buf[first : first + slots, :DC] = lat_ref[...]
    key_buf[first : first + slots, DC:] = masked_rope(note_ref, slots)


def masked_rope(note_ref, slots):
    part = note_ref.shape[0] - GROUP - DR // 2
    lane = part // GROUP * LANES
    live = note_ref[part : part + 1, lane : lane + 1].astype(F32)
    blocked = jnp.where(iota((LANES - DR, slots), 1).astype(F32) < live, 0.0, BLOCKED)
    blocked = jnp.where(iota((LANES - DR, slots), 0) == 0, blocked, 0.0)
    rope = note_ref[part + GROUP :, :].astype(F32)
    return jnp.concatenate([rope[:, :slots], rope[:, slots:], blocked], axis=0).T.astype(BF16)


def put_fresh(key_buf, first, note_refs):
    part = note_refs[0].shape[0] - GROUP - DR // 2
    for index, note_ref in enumerate(note_refs):
        key_buf[first + index * part : first + (index + 1) * part, :DC] = note_ref[:part, :]
        for k in range(part // GROUP):
            rows = span(k, GROUP, first + index * part)
            key_buf[rows, DC:] = note_ref[part : part + GROUP, k * LANES : (k + 1) * LANES]


def causal(part, blocks):
    count = part * blocks
    me = lax.axis_index("ctx")
    col = iota((count, count), 1)
    origin = jnp.bitwise_xor(jnp.full((count, count), me, jnp.int32), col // part)
    return jnp.where(origin * part + col % part <= iota((count, count), 0), 0.0, BLOCKED)


def pipeline(steps, scores, weigh, collect):
    upcoming, previous = scores(0), None
    for step in range(steps):
        now = upcoming
        if step + 1 < steps:
            upcoming = scores(step + 1)
        if previous is not None:
            collect(step - 1, *previous)
        previous = weigh(step, now)
    collect(steps - 1, *previous)


def exponents(s, level, total):
    parts = []
    for k in range(s.shape[1] // LANES):
        p = jnp.exp2((s[:, k * LANES : (k + 1) * LANES] - level) * EXP_SCALE)
        total = p if total is None else total + p
        parts.append(p.astype(BF16))
    return jnp.concatenate(parts, axis=1), total


def state_shapes(rows):
    return (pltpu.VMEM((rows, DV), F32), pltpu.VMEM((rows, LANES), F32), pltpu.VMEM((rows, LANES), F32))


def near_kernel(q_ref, *refs, cached, size):
    w_hbm, out_ref, sum_ref, max_ref, w_ref, key_buf, sem = refs[2 * cached :]
    copy = pltpu.make_async_copy(w_hbm, w_ref, sem)
    copy.start()
    slots = refs[0].shape[0]
    for k in range(cached):
        put_cached(key_buf, k * slots, refs[2 * k], refs[2 * k + 1])
    count = size // HEADS_STEP

    def scores(step):
        q = q_ref[span(step, size), :]
        return jnp.concatenate([dot_t(q, key_buf[span(k, slots), :]) for k in range(cached)], axis=1)

    def weigh(step, s):
        level = jnp.max(s, axis=1, keepdims=True)
        p, total = exponents(s, level, None)
        sum_ref[span(step, size), :] = total
        max_ref[span(step, size), :] = jnp.broadcast_to(level, (size, LANES))
        return (p,)

    def collect(step, p):
        mixed = dot(p, key_buf[:, :DC]).astype(BF16)
        if step == 0:
            copy.wait()
        for k in range(HEADS_STEP):
            head = step * HEADS_STEP + k
            out_ref[span(head, count), :] = dot(mixed[span(k, count), :], w_ref[:, span(head, DV)])

    pipeline(q_ref.shape[0] // size, scores, weigh, collect)


def near_pass(q, blocks, w_value, count):
    rows = q.shape[0]
    keys = sum(block[0].shape[0] for block in blocks)
    return pl.pallas_call(
        functools.partial(near_kernel, cached=len(blocks), size=HEADS_STEP * count),
        out_shape=(*state_shapes(rows), pltpu.VMEM(w_value.shape, BF16)),
        in_specs=[VMEM] * (1 + 2 * len(blocks)) + [HBM],
        out_specs=(VMEM, VMEM, VMEM, VMEM),
        scratch_shapes=[pltpu.VMEM((keys, KEY), BF16), pltpu.SemaphoreType.DMA],
        compiler_params=params(),
        cost_estimate=cost(COSTS["near_rows"]),
        name="near_rows",
    )(q, *[array for block in blocks for array in block], in_hbm(w_value))


def early_kernel(q_ref, lat_ref, w_ref, out_ref, value_ref, *, size):
    for step in range(q_ref.shape[0] // size):
        rows = span(step, size)
        out_ref[rows, :] = dot_t(q_ref[rows, :DC], lat_ref[...])
        cols = span(step, HEADS_STEP * DV)
        value_ref[:, cols] = dot(lat_ref[...], w_ref[:, cols]).astype(BF16)


def early_pass(q, lat, w_value, count):
    rows = q.shape[0]
    slots = lat.shape[0]
    return pl.pallas_call(
        functools.partial(early_kernel, size=HEADS_STEP * count),
        out_shape=(pltpu.VMEM((rows, slots), F32), pltpu.VMEM((slots, w_value.shape[1]), BF16)),
        in_specs=[VMEM] * 3,
        out_specs=(VMEM, VMEM),
        compiler_params=params(),
        cost_estimate=cost(COSTS["early"]),
        name="early",
    )(q, lat, w_value)


def far_kernel(
    q_ref,
    note_ref,
    s_ref,
    value_ref,
    out_in,
    sum_in,
    max_in,
    lat_ref,
    w_ref,
    out_ref,
    sum_ref,
    max_ref,
    next_ref,
    ext_buf,
    *,
    size,
):
    ext_buf[...] = masked_rope(note_ref, value_ref.shape[0])
    count = size // HEADS_STEP

    def scores(step):
        rows = span(step, size)
        return s_ref[rows, :] + dot_t(q_ref[rows, DC:], ext_buf[...])

    def weigh(step, s):
        rows = span(step, size)
        before = max_in[rows, :]
        level = jnp.maximum(before, jnp.max(s, axis=1, keepdims=True))
        factor = jnp.exp2((before - level) * EXP_SCALE)
        p, total = exponents(s, level, sum_in[rows, :] * factor)
        sum_ref[rows, :] = total
        max_ref[rows, :] = level
        cols = span(step, HEADS_STEP * DV)
        next_ref[:, cols] = dot(lat_ref[...], w_ref[:, cols]).astype(BF16)
        return p, factor

    def collect(step, p, factor):
        for k in range(HEADS_STEP):
            head = step * HEADS_STEP + k
            grown = dot(p[span(k, count), :], value_ref[:, span(head, DV)])
            out_ref[span(head, count), :] = out_in[span(head, count), :] * factor[span(k, count), :] + grown

    pipeline(q_ref.shape[0] // size, scores, weigh, collect)


def far_pass(q, note, scores, values, state, next_lat, w_value, count):
    rows = q.shape[0]
    return pl.pallas_call(
        functools.partial(far_kernel, size=HEADS_STEP * count),
        out_shape=(*state_shapes(rows), pltpu.VMEM((next_lat.shape[0], w_value.shape[1]), BF16)),
        in_specs=[VMEM] * 9,
        out_specs=(VMEM, VMEM, VMEM, VMEM),
        scratch_shapes=[pltpu.VMEM((values.shape[0], LANES), BF16)],
        compiler_params=params(),
        cost_estimate=cost(COSTS["far_rows"]),
        name="far_rows",
    )(q, note, scores, values, *state, next_lat, w_value)


def last_kernel(q_ref, lat_ref, value_ref, *refs, blocks, size):
    notes, refs = refs[:blocks], refs[blocks:]
    out_in, sum_in, max_in, w_ref, out_hbm, key_buf, out_buf, sems = refs
    slots = lat_ref.shape[0]
    count = out_hbm.shape[0]
    put_fresh(key_buf, slots, notes)
    put_cached(key_buf, 0, lat_ref, notes[-1])
    bias = jnp.concatenate([causal(count // blocks, blocks)] * HEADS_STEP, axis=0)
    copies = []

    def scores(step):
        q = q_ref[span(step, size), :]
        fresh = dot_t(q, key_buf[slots:, :]) + bias
        return jnp.concatenate([dot_t(q, key_buf[:slots, :]), fresh], axis=1)

    def weigh(step, s):
        rows = span(step, size)
        before = max_in[rows, :]
        level = jnp.maximum(before, jnp.max(s, axis=1, keepdims=True))
        factor = jnp.exp2((before - level) * EXP_SCALE)
        p, total = exponents(s, level, sum_in[rows, :] * factor)
        inverse = 1.0 / jnp.sum(total, axis=1, keepdims=True)
        fresh = dot(key_buf[slots:, :DC], w_ref[:, span(step, HEADS_STEP * DV)]).astype(BF16)
        return p, factor * inverse, inverse, fresh

    def collect(step, p, factor, inverse, fresh):
        for k in range(HEADS_STEP):
            head = step * HEADS_STEP + k
            part = span(k, count)
            grown = dot(p[part, :slots], value_ref[:, span(head, DV)]) + dot(p[part, slots:], fresh[:, span(k, DV)])
            whole = out_in[span(head, count), :] * factor[part, :] + grown * inverse[part, :]
            out_buf[:, span(head, DV)] = whole.astype(BF16)
        cols = span(step, HEADS_STEP * DV)
        copies.append(pltpu.make_async_copy(out_buf.at[:, cols], out_hbm.at[:, cols], sems.at[step]))
        copies[-1].start()

    pipeline(q_ref.shape[0] // size, scores, weigh, collect)
    for copy in copies:
        copy.wait()


def last_pass(q, lat, values, notes, state, w_value, count):
    rows = q.shape[0]
    shape = (count, w_value.shape[1])
    return pl.pallas_call(
        functools.partial(last_kernel, blocks=len(notes), size=HEADS_STEP * count),
        out_shape=jax.ShapeDtypeStruct(shape, BF16),
        in_specs=[VMEM] * (7 + len(notes)),
        out_specs=HBM,
        scratch_shapes=[
            pltpu.VMEM((lat.shape[0] + count, KEY), BF16),
            pltpu.VMEM(shape, BF16),
            pltpu.SemaphoreType.DMA((rows // (HEADS_STEP * count),)),
        ],
        compiler_params=params(),
        cost_estimate=cost(COSTS["last_rows"]),
        name="last_rows",
    )(q, lat, values, *notes, *state, w_value)


def hop(array, bit):
    size = lax.axis_size("ctx")
    return lax.ppermute(array, "ctx", [(k, k ^ bit) for k in range(size)])


def shards(q_nope, q_rope, cache_latent, cache_rope, new_latent, new_rope, lengths, w_key, w_value):
    count = q_nope.shape[1]
    lat = cache_latent[0]
    far_lat, near_lat = hop(lat, 2), hop(lat, 1)
    heads = w_key.shape[1] // DH
    note, lat, own_q, own_r = pack(
        new_latent[0], new_rope[0], cache_rope[0].T, lat, q_nope, q_rope, lengths, heads
    )
    near_note = hop(note, 1)
    q = make_queries(own_q, own_r, w_key)
    far_note = hop(note, 2)
    *state, w_value = near_pass(q, [(lat, note), (near_lat, near_note)], w_value, count)
    last_lat = hop(after(far_lat, state[2]), 1)
    scores, values = early_pass(q, far_lat, w_value, count)
    last_note = hop(after(far_note, scores), 1)
    *state, values = far_pass(q, far_note, scores, values, state, last_lat, w_value, count)
    notes = [note, near_note, far_note, last_note]
    return last_pass(q, last_lat, values, notes, state, w_value, count)[None]


def solution(mesh):
    return jax.shard_map(
        shards,
        mesh=mesh,
        in_specs=(
            P("req", None, None),
            P("req", None, None),
            P("req", "ctx", None),
            P("req", "ctx", None),
            P("req", "ctx", None),
            P("req", "ctx", None),
            P("req", "ctx"),
            P(None, "ctx"),
            P(None, "ctx"),
        ),
        out_specs=P("req", None, "ctx"),
        check_vma=False,
    )
```

```python
import functools
import math

import jax
import jax.numpy as jnp
from jax import lax
from jax.experimental import pallas as pl
from jax.experimental.pallas import tpu as pltpu
from jax.sharding import PartitionSpec as P

DC = 512
DR = 64
DH = 128
DV = 128
LANES = 128
KEY = DC + LANES
BLOCKED = -1e30
EXP_SCALE = math.log2(math.e) / math.sqrt(DH + DR)
HEADS_STEP = 4
HEADS_LAST = 8
GROUP = 16
COSTS = {"pack": 0.6, "latent_queries": 0.001, "pass_on": 0.001, "near_rows": 1.0, "early": 3.0, "far_rows": 3.0, "last_rows": 0.001}
VMEM_LIMIT = 20 * 1024 * 1024


def cost(micros):
    return pl.CostEstimate(flops=int(micros * 1e9), bytes_accessed=1024, transcendentals=0)


BF16 = jnp.bfloat16
F32 = jnp.float32

VMEM = pl.BlockSpec(memory_space=pltpu.VMEM)
HBM = pl.BlockSpec(memory_space=pltpu.HBM)
ANYWHERE = pl.BlockSpec(memory_space=pl.ANY)


def iota(shape, dim):
    return lax.broadcasted_iota(jnp.int32, shape, dim)


def span(step, size, first=0):
    return slice(first + step * size, first + (step + 1) * size)


def params():
    return pltpu.CompilerParams(vmem_limit_bytes=VMEM_LIMIT)


def in_vmem(array):
    return pltpu.with_memory_space_constraint(array, pltpu.VMEM)


def dot(a, b):
    return jnp.dot(a, b, preferred_element_type=F32)


def dot_t(a, b):
    return lax.dot_general(a, b, (((1,), (1,)), ((), ())), preferred_element_type=F32)


def in_hbm(array):
    return pltpu.with_memory_space_constraint(array, pltpu.HBM)


def pack_kernel(
    fresh_hbm,
    rope_hbm,
    cached_hbm,
    lat_hbm,
    q_hbm,
    r_hbm,
    length_ref,
    note_ref,
    lat_ref,
    q_ref,
    r_ref,
    rope_buf,
    cached_buf,
    sems,
):
    part = fresh_hbm.shape[0]
    slots = cached_hbm.shape[1]
    me = lax.axis_index("ctx")
    q_first = pl.multiple_of(me * q_ref.shape[1], LANES)
    r_first = pl.multiple_of(me * r_ref.shape[1], LANES)
    pairs = [
        (rope_hbm, rope_buf),
        (cached_hbm, cached_buf),
        (fresh_hbm, note_ref.at[:part, :]),
        (q_hbm.at[0, :, pl.ds(q_first, q_ref.shape[1])], q_ref),
        (r_hbm.at[0, :, pl.ds(r_first, r_ref.shape[1])], r_ref),
        (lat_hbm, lat_ref),
    ]
    copies = [pltpu.make_async_copy(source, target, sems.at[k]) for k, (source, target) in enumerate(pairs)]
    for copy in copies:
        copy.start()
    groups = part // GROUP
    note_ref[part : part + GROUP, :] = jnp.zeros((GROUP, DC), BF16)
    live = jnp.broadcast_to(length_ref[...], (GROUP, LANES)).astype(F32).astype(BF16)
    note_ref[part : part + GROUP, groups * LANES : (groups + 1) * LANES] = live
    copies[0].wait()
    for k in range(groups):
        note_ref[part : part + GROUP, k * LANES : k * LANES + DR] = rope_buf[span(k, GROUP), :]
    copies[1].wait()
    note_ref[part + GROUP :, :slots] = cached_buf[: DR // 2, :]
    note_ref[part + GROUP :, slots:] = cached_buf[DR // 2 :, :]
    for copy in copies[2:]:
        copy.wait()


def pack(fresh, rope, cached_rope, lat, q_nope, q_rope, length, heads):
    part = fresh.shape[0]
    count = q_nope.shape[1]
    return pl.pallas_call(
        pack_kernel,
        out_shape=(
            pltpu.VMEM((part + GROUP + DR // 2, DC), BF16),
            pltpu.VMEM(lat.shape, BF16),
            pltpu.VMEM((count, heads * DH), BF16),
            pltpu.VMEM((count, heads * DR), BF16),
        ),
        in_specs=[HBM] * 6 + [VMEM],
        out_specs=(VMEM, VMEM, VMEM, VMEM),
        scratch_shapes=[
            pltpu.VMEM(rope.shape, BF16),
            pltpu.VMEM(cached_rope.shape, BF16),
            pltpu.SemaphoreType.DMA((6,)),
        ],
        compiler_params=params(),
        cost_estimate=cost(COSTS["pack"]),
        name="pack",
    )(*[in_hbm(array) for array in (fresh, rope, cached_rope, lat, q_nope, q_rope)], length)


def queries_kernel(q_ref, r_ref, w_ref, out_ref):
    count = q_ref.shape[0]
    heads = out_ref.shape[0] // count
    lane = iota((count, LANES), 1)
    side = jnp.where(lane == DR, 1.0, 0.0)
    for pair in range(heads // 2):
        both = r_ref[:, span(pair, LANES)].astype(F32)
        for odd in range(2):
            head = 2 * pair + odd
            one = pltpu.roll(both, DR, 1) if odd else both
            out_ref[span(head, count), :DC] = dot_t(q_ref[:, span(head, DH)], w_ref[:, span(head, DH)]).astype(BF16)
            out_ref[span(head, count), DC:] = jnp.where(lane < DR, one, side).astype(BF16)


def make_queries(q, r, w_key):
    count = q.shape[0]
    heads = w_key.shape[1] // DH
    return pl.pallas_call(
        queries_kernel,
        out_shape=pltpu.VMEM((heads * count, KEY), BF16),
        in_specs=[VMEM] * 3,
        out_specs=VMEM,
        compiler_params=params(),
        cost_estimate=cost(COSTS["latent_queries"]),
        name="latent_queries",
    )(q, r, in_vmem(w_key))


def pass_kernel(array_ref, token_ref, out_ref):
    out_ref[...] = array_ref[...]


def after(array, token):
    return pl.pallas_call(
        pass_kernel,
        out_shape=pltpu.VMEM(array.shape, BF16),
        in_specs=[VMEM, ANYWHERE],
        out_specs=VMEM,
        compiler_params=params(),
        cost_estimate=cost(COSTS["pass_on"]),
        name="pass_on",
    )(array, token)


def put_cached(key_buf, first, lat_ref, note_ref):
    slots = lat_ref.shape[0]
    key_buf[first : first + slots, :DC] = lat_ref[...]
    key_buf[first : first + slots, DC:] = masked_rope(note_ref, slots)


def masked_rope(note_ref, slots):
    part = note_ref.shape[0] - GROUP - DR // 2
    lane = part // GROUP * LANES
    live = note_ref[part : part + 1, lane : lane + 1].astype(F32)
    blocked = jnp.where(iota((LANES - DR, slots), 1).astype(F32) < live, 0.0, BLOCKED)
    blocked = jnp.where(iota((LANES - DR, slots), 0) == 0, blocked, 0.0)
    rope = note_ref[part + GROUP :, :].astype(F32)
    return jnp.concatenate([rope[:, :slots], rope[:, slots:], blocked], axis=0).T.astype(BF16)


def put_fresh(key_buf, first, note_refs):
    part = note_refs[0].shape[0] - GROUP - DR // 2
    for index, note_ref in enumerate(note_refs):
        key_buf[first + index * part : first + (index + 1) * part, :DC] = note_ref[:part, :]
        for k in range(part // GROUP):
            rows = span(k, GROUP, first + index * part)
            key_buf[rows, DC:] = note_ref[part : part + GROUP, k * LANES : (k + 1) * LANES]


def causal(part, blocks):
    count = part * blocks
    me = lax.axis_index("ctx")
    col = iota((count, count), 1)
    origin = jnp.bitwise_xor(jnp.full((count, count), me, jnp.int32), col // part)
    return jnp.where(origin * part + col % part <= iota((count, count), 0), 0.0, BLOCKED)


def pipeline(steps, scores, weigh, collect):
    upcoming, previous = scores(0), None
    for step in range(steps):
        now = upcoming
        if step + 1 < steps:
            upcoming = scores(step + 1)
        if previous is not None:
            collect(step - 1, *previous)
        previous = weigh(step, now)
    collect(steps - 1, *previous)


def exponents(s, level, total):
    parts = []
    for k in range(s.shape[1] // LANES):
        p = jnp.exp2((s[:, k * LANES : (k + 1) * LANES] - level) * EXP_SCALE)
        total = p if total is None else total + p
        parts.append(p.astype(BF16))
    return jnp.concatenate(parts, axis=1), total


def state_shapes(rows):
    return (pltpu.VMEM((rows, DV), F32), pltpu.VMEM((rows, LANES), F32), pltpu.VMEM((rows, LANES), F32))


def near_kernel(q_ref, *refs, cached, size):
    w_hbm, out_ref, sum_ref, max_ref, w_ref, key_buf, sem = refs[2 * cached :]
    copy = pltpu.make_async_copy(w_hbm, w_ref, sem)
    copy.start()
    slots = refs[0].shape[0]
    for k in range(cached):
        put_cached(key_buf, k * slots, refs[2 * k], refs[2 * k + 1])
    count = size // HEADS_STEP

    def scores(step):
        q = q_ref[span(step, size), :]
        return jnp.concatenate([dot_t(q, key_buf[span(k, slots), :]) for k in range(cached)], axis=1)

    def weigh(step, s):
        level = jnp.max(s, axis=1, keepdims=True)
        p, total = exponents(s, level, None)
        sum_ref[span(step, size), :] = total
        max_ref[span(step, size), :] = jnp.broadcast_to(level, (size, LANES))
        return (p,)

    def collect(step, p):
        mixed = dot(p, key_buf[:, :DC]).astype(BF16)
        if step == 0:
            copy.wait()
        for k in range(HEADS_STEP):
            head = step * HEADS_STEP + k
            out_ref[span(head, count), :] = dot(mixed[span(k, count), :], w_ref[:, span(head, DV)])

    pipeline(q_ref.shape[0] // size, scores, weigh, collect)


def near_pass(q, blocks, w_value, count):
    rows = q.shape[0]
    keys = sum(block[0].shape[0] for block in blocks)
    return pl.pallas_call(
        functools.partial(near_kernel, cached=len(blocks), size=HEADS_STEP * count),
        out_shape=(*state_shapes(rows), pltpu.VMEM(w_value.shape, BF16)),
        in_specs=[VMEM] * (1 + 2 * len(blocks)) + [HBM],
        out_specs=(VMEM, VMEM, VMEM, VMEM),
        scratch_shapes=[pltpu.VMEM((keys, KEY), BF16), pltpu.SemaphoreType.DMA],
        compiler_params=params(),
        cost_estimate=cost(COSTS["near_rows"]),
        name="near_rows",
    )(q, *[array for block in blocks for array in block], in_hbm(w_value))


def early_kernel(q_ref, lat_ref, w_ref, out_ref, value_ref, *, size):
    for step in range(q_ref.shape[0] // size):
        rows = span(step, size)
        out_ref[rows, :] = dot_t(q_ref[rows, :DC], lat_ref[...])
        cols = span(step, HEADS_STEP * DV)
        value_ref[:, cols] = dot(lat_ref[...], w_ref[:, cols]).astype(BF16)


def early_pass(q, lat, w_value, count):
    rows = q.shape[0]
    slots = lat.shape[0]
    return pl.pallas_call(
        functools.partial(early_kernel, size=HEADS_STEP * count),
        out_shape=(pltpu.VMEM((rows, slots), F32), pltpu.VMEM((slots, w_value.shape[1]), BF16)),
        in_specs=[VMEM] * 3,
        out_specs=(VMEM, VMEM),
        compiler_params=params(),
        cost_estimate=cost(COSTS["early"]),
        name="early",
    )(q, lat, w_value)


def far_kernel(
    q_ref,
    note_ref,
    s_ref,
    value_ref,
    out_in,
    sum_in,
    max_in,
    lat_ref,
    w_ref,
    out_ref,
    sum_ref,
    max_ref,
    next_ref,
    ext_buf,
    *,
    size,
):
    ext_buf[...] = masked_rope(note_ref, value_ref.shape[0])
    count = size // HEADS_STEP

    def scores(step):
        rows = span(step, size)
        return s_ref[rows, :] + dot_t(q_ref[rows, DC:], ext_buf[...])

    def weigh(step, s):
        rows = span(step, size)
        before = max_in[rows, :]
        level = jnp.maximum(before, jnp.max(s, axis=1, keepdims=True))
        factor = jnp.exp2((before - level) * EXP_SCALE)
        p, total = exponents(s, level, sum_in[rows, :] * factor)
        sum_ref[rows, :] = total
        max_ref[rows, :] = level
        cols = span(step, HEADS_STEP * DV)
        next_ref[:, cols] = dot(lat_ref[...], w_ref[:, cols]).astype(BF16)
        return p, factor

    def collect(step, p, factor):
        for k in range(HEADS_STEP):
            head = step * HEADS_STEP + k
            grown = dot(p[span(k, count), :], value_ref[:, span(head, DV)])
            out_ref[span(head, count), :] = out_in[span(head, count), :] * factor[span(k, count), :] + grown

    pipeline(q_ref.shape[0] // size, scores, weigh, collect)


def far_pass(q, note, scores, values, state, next_lat, w_value, count):
    rows = q.shape[0]
    return pl.pallas_call(
        functools.partial(far_kernel, size=HEADS_STEP * count),
        out_shape=(*state_shapes(rows), pltpu.VMEM((next_lat.shape[0], w_value.shape[1]), BF16)),
        in_specs=[VMEM] * 9,
        out_specs=(VMEM, VMEM, VMEM, VMEM),
        scratch_shapes=[pltpu.VMEM((values.shape[0], LANES), BF16)],
        compiler_params=params(),
        cost_estimate=cost(COSTS["far_rows"]),
        name="far_rows",
    )(q, note, scores, values, *state, next_lat, w_value)


def last_kernel(q_ref, lat_ref, value_ref, *refs, blocks, size):
    notes, refs = refs[:blocks], refs[blocks:]
    out_in, sum_in, max_in, w_ref, out_hbm, key_buf, out_buf, sems = refs
    slots = lat_ref.shape[0]
    count = out_hbm.shape[0]
    put_fresh(key_buf, slots, notes)
    put_cached(key_buf, 0, lat_ref, notes[-1])
    bias = jnp.concatenate([causal(count // blocks, blocks)] * HEADS_LAST, axis=0)
    copies = []

    def scores(step):
        q = q_ref[span(step, size), :]
        fresh = dot_t(q, key_buf[slots:, :]) + bias
        return jnp.concatenate([dot_t(q, key_buf[:slots, :]), fresh], axis=1)

    def weigh(step, s):
        rows = span(step, size)
        before = max_in[rows, :]
        level = jnp.maximum(before, jnp.max(s, axis=1, keepdims=True))
        factor = jnp.exp2((before - level) * EXP_SCALE)
        p, total = exponents(s, level, sum_in[rows, :] * factor)
        inverse = 1.0 / jnp.sum(total, axis=1, keepdims=True)
        fresh = dot(key_buf[slots:, :DC], w_ref[:, span(step, HEADS_LAST * DV)]).astype(BF16)
        return p, factor * inverse, inverse, fresh

    def collect(step, p, factor, inverse, fresh):
        for k in range(HEADS_LAST):
            head = step * HEADS_LAST + k
            part = span(k, count)
            grown = dot(p[part, :slots], value_ref[:, span(head, DV)]) + dot(p[part, slots:], fresh[:, span(k, DV)])
            whole = out_in[span(head, count), :] * factor[part, :] + grown * inverse[part, :]
            out_buf[:, span(head, DV)] = whole.astype(BF16)
        cols = span(step, HEADS_LAST * DV)
        copies.append(pltpu.make_async_copy(out_buf.at[:, cols], out_hbm.at[:, cols], sems.at[step]))
        copies[-1].start()

    pipeline(q_ref.shape[0] // size, scores, weigh, collect)
    for copy in copies:
        copy.wait()


def last_pass(q, lat, values, notes, state, w_value, count):
    rows = q.shape[0]
    shape = (count, w_value.shape[1])
    return pl.pallas_call(
        functools.partial(last_kernel, blocks=len(notes), size=HEADS_LAST * count),
        out_shape=jax.ShapeDtypeStruct(shape, BF16),
        in_specs=[VMEM] * (7 + len(notes)),
        out_specs=HBM,
        scratch_shapes=[
            pltpu.VMEM((lat.shape[0] + count, KEY), BF16),
            pltpu.VMEM(shape, BF16),
            pltpu.SemaphoreType.DMA((rows // (HEADS_LAST * count),)),
        ],
        compiler_params=params(),
        cost_estimate=cost(COSTS["last_rows"]),
        name="last_rows",
    )(q, lat, values, *notes, *state, w_value)


def hop(array, bit):
    size = lax.axis_size("ctx")
    return lax.ppermute(array, "ctx", [(k, k ^ bit) for k in range(size)])


def shards(q_nope, q_rope, cache_latent, cache_rope, new_latent, new_rope, lengths, w_key, w_value):
    count = q_nope.shape[1]
    lat = cache_latent[0]
    far_lat, near_lat = hop(lat, 2), hop(lat, 1)
    heads = w_key.shape[1] // DH
    note, lat, own_q, own_r = pack(
        new_latent[0], new_rope[0], cache_rope[0].T, lat, q_nope, q_rope, lengths, heads
    )
    near_note = hop(note, 1)
    q = make_queries(own_q, own_r, w_key)
    far_note = hop(note, 2)
    *state, w_value = near_pass(q, [(lat, note), (near_lat, near_note)], w_value, count)
    last_lat = hop(after(far_lat, state[2]), 1)
    scores, values = early_pass(q, far_lat, w_value, count)
    last_note = hop(after(far_note, scores), 1)
    *state, values = far_pass(q, far_note, scores, values, state, last_lat, w_value, count)
    notes = [note, near_note, far_note, last_note]
    return last_pass(q, last_lat, values, notes, state, w_value, count)[None]


def solution(mesh):
    return jax.shard_map(
        shards,
        mesh=mesh,
        in_specs=(
            P("req", None, None),
            P("req", None, None),
            P("req", "ctx", None),
            P("req", "ctx", None),
            P("req", "ctx", None),
            P("req", "ctx", None),
            P("req", "ctx"),
            P(None, "ctx"),
            P(None, "ctx"),
        ),
        out_specs=P("req", None, "ctx"),
        check_vma=False,
    )
```

```python
import functools
import math

import jax
import jax.numpy as jnp
from jax import lax
from jax.experimental import pallas as pl
from jax.experimental.pallas import tpu as pltpu
from jax.sharding import PartitionSpec as P

DC = 512
DR = 64
DH = 128
DV = 128
LANES = 128
KEY = DC + LANES
BLOCKED = -1e30
EXP_SCALE = math.log2(math.e) / math.sqrt(DH + DR)
HEADS_STEP = 4
HEADS_LAST = 8
HEADS_SENT = 2
GROUP = 16
COSTS = {"pack": 0.6, "latent_queries": 0.001, "pass_on": 0.001, "near_rows": 1.0, "early": 3.0, "far_rows": 3.0, "last_rows": 0.001}
VMEM_LIMIT = 20 * 1024 * 1024


def cost(micros):
    return pl.CostEstimate(flops=int(micros * 1e9), bytes_accessed=1024, transcendentals=0)


BF16 = jnp.bfloat16
F32 = jnp.float32

VMEM = pl.BlockSpec(memory_space=pltpu.VMEM)
HBM = pl.BlockSpec(memory_space=pltpu.HBM)
ANYWHERE = pl.BlockSpec(memory_space=pl.ANY)


def iota(shape, dim):
    return lax.broadcasted_iota(jnp.int32, shape, dim)


def span(step, size, first=0):
    return slice(first + step * size, first + (step + 1) * size)


def params():
    return pltpu.CompilerParams(vmem_limit_bytes=VMEM_LIMIT)


def in_vmem(array):
    return pltpu.with_memory_space_constraint(array, pltpu.VMEM)


def dot(a, b):
    return jnp.dot(a, b, preferred_element_type=F32)


def dot_t(a, b):
    return lax.dot_general(a, b, (((1,), (1,)), ((), ())), preferred_element_type=F32)


def in_hbm(array):
    return pltpu.with_memory_space_constraint(array, pltpu.HBM)


def pack_kernel(
    fresh_hbm,
    rope_hbm,
    cached_hbm,
    lat_hbm,
    q_hbm,
    r_hbm,
    length_ref,
    note_ref,
    lat_ref,
    q_ref,
    r_ref,
    rope_buf,
    cached_buf,
    sems,
):
    part = fresh_hbm.shape[0]
    slots = cached_hbm.shape[1]
    me = lax.axis_index("ctx")
    q_first = pl.multiple_of(me * q_ref.shape[1], LANES)
    r_first = pl.multiple_of(me * r_ref.shape[1], LANES)
    pairs = [
        (rope_hbm, rope_buf),
        (cached_hbm, cached_buf),
        (fresh_hbm, note_ref.at[:part, :]),
        (q_hbm.at[0, :, pl.ds(q_first, q_ref.shape[1])], q_ref),
        (r_hbm.at[0, :, pl.ds(r_first, r_ref.shape[1])], r_ref),
        (lat_hbm, lat_ref),
    ]
    copies = [pltpu.make_async_copy(source, target, sems.at[k]) for k, (source, target) in enumerate(pairs)]
    for copy in copies:
        copy.start()
    groups = part // GROUP
    note_ref[part : part + GROUP, :] = jnp.zeros((GROUP, DC), BF16)
    live = jnp.broadcast_to(length_ref[...], (GROUP, LANES)).astype(F32).astype(BF16)
    note_ref[part : part + GROUP, groups * LANES : (groups + 1) * LANES] = live
    copies[0].wait()
    for k in range(groups):
        note_ref[part : part + GROUP, k * LANES : k * LANES + DR] = rope_buf[span(k, GROUP), :]
    copies[1].wait()
    note_ref[part + GROUP :, :slots] = cached_buf[: DR // 2, :]
    note_ref[part + GROUP :, slots:] = cached_buf[DR // 2 :, :]
    for copy in copies[2:]:
        copy.wait()


def pack(fresh, rope, cached_rope, lat, q_nope, q_rope, length, heads):
    part = fresh.shape[0]
    count = q_nope.shape[1]
    return pl.pallas_call(
        pack_kernel,
        out_shape=(
            pltpu.VMEM((part + GROUP + DR // 2, DC), BF16),
            pltpu.VMEM(lat.shape, BF16),
            pltpu.VMEM((count, heads * DH), BF16),
            pltpu.VMEM((count, heads * DR), BF16),
        ),
        in_specs=[HBM] * 6 + [VMEM],
        out_specs=(VMEM, VMEM, VMEM, VMEM),
        scratch_shapes=[
            pltpu.VMEM(rope.shape, BF16),
            pltpu.VMEM(cached_rope.shape, BF16),
            pltpu.SemaphoreType.DMA((6,)),
        ],
        compiler_params=params(),
        cost_estimate=cost(COSTS["pack"]),
        name="pack",
    )(*[in_hbm(array) for array in (fresh, rope, cached_rope, lat, q_nope, q_rope)], length)


def queries_kernel(q_ref, r_ref, w_ref, out_ref):
    count = q_ref.shape[0]
    heads = out_ref.shape[0] // count
    lane = iota((count, LANES), 1)
    side = jnp.where(lane == DR, 1.0, 0.0)
    for pair in range(heads // 2):
        both = r_ref[:, span(pair, LANES)].astype(F32)
        for odd in range(2):
            head = 2 * pair + odd
            one = pltpu.roll(both, DR, 1) if odd else both
            out_ref[span(head, count), :DC] = dot_t(q_ref[:, span(head, DH)], w_ref[:, span(head, DH)]).astype(BF16)
            out_ref[span(head, count), DC:] = jnp.where(lane < DR, one, side).astype(BF16)


def make_queries(q, r, w_key):
    count = q.shape[0]
    heads = w_key.shape[1] // DH
    return pl.pallas_call(
        queries_kernel,
        out_shape=pltpu.VMEM((heads * count, KEY), BF16),
        in_specs=[VMEM] * 3,
        out_specs=VMEM,
        compiler_params=params(),
        cost_estimate=cost(COSTS["latent_queries"]),
        name="latent_queries",
    )(q, r, in_vmem(w_key))


def pass_kernel(array_ref, token_ref, out_ref):
    out_ref[...] = array_ref[...]


def after(array, token):
    return pl.pallas_call(
        pass_kernel,
        out_shape=pltpu.VMEM(array.shape, BF16),
        in_specs=[VMEM, ANYWHERE],
        out_specs=VMEM,
        compiler_params=params(),
        cost_estimate=cost(COSTS["pass_on"]),
        name="pass_on",
    )(array, token)


def put_cached(key_buf, first, lat_ref, note_ref):
    slots = lat_ref.shape[0]
    key_buf[first : first + slots, :DC] = lat_ref[...]
    key_buf[first : first + slots, DC:] = masked_rope(note_ref, slots)


def masked_rope(note_ref, slots):
    part = note_ref.shape[0] - GROUP - DR // 2
    lane = part // GROUP * LANES
    live = note_ref[part : part + 1, lane : lane + 1].astype(F32)
    blocked = jnp.where(iota((LANES - DR, slots), 1).astype(F32) < live, 0.0, BLOCKED)
    blocked = jnp.where(iota((LANES - DR, slots), 0) == 0, blocked, 0.0)
    rope = note_ref[part + GROUP :, :].astype(F32)
    return jnp.concatenate([rope[:, :slots], rope[:, slots:], blocked], axis=0).T.astype(BF16)


def put_fresh(key_buf, first, note_refs):
    part = note_refs[0].shape[0] - GROUP - DR // 2
    for index, note_ref in enumerate(note_refs):
        key_buf[first + index * part : first + (index + 1) * part, :DC] = note_ref[:part, :]
        for k in range(part // GROUP):
            rows = span(k, GROUP, first + index * part)
            key_buf[rows, DC:] = note_ref[part : part + GROUP, k * LANES : (k + 1) * LANES]


def causal(part, blocks):
    count = part * blocks
    me = lax.axis_index("ctx")
    col = iota((count, count), 1)
    origin = jnp.bitwise_xor(jnp.full((count, count), me, jnp.int32), col // part)
    return jnp.where(origin * part + col % part <= iota((count, count), 0), 0.0, BLOCKED)


def pipeline(steps, scores, weigh, collect):
    upcoming, previous = scores(0), None
    for step in range(steps):
        now = upcoming
        if step + 1 < steps:
            upcoming = scores(step + 1)
        if previous is not None:
            collect(step - 1, *previous)
        previous = weigh(step, now)
    collect(steps - 1, *previous)


def exponents(s, level, total):
    parts = []
    for k in range(s.shape[1] // LANES):
        p = jnp.exp2((s[:, k * LANES : (k + 1) * LANES] - level) * EXP_SCALE)
        total = p if total is None else total + p
        parts.append(p.astype(BF16))
    return jnp.concatenate(parts, axis=1), total


def state_shapes(rows):
    return (pltpu.VMEM((rows, DV), F32), pltpu.VMEM((rows, LANES), F32), pltpu.VMEM((rows, LANES), F32))


def near_kernel(q_ref, *refs, cached, size):
    w_hbm, out_ref, sum_ref, max_ref, w_ref, key_buf, sem = refs[2 * cached :]
    copy = pltpu.make_async_copy(w_hbm, w_ref, sem)
    copy.start()
    slots = refs[0].shape[0]
    for k in range(cached):
        put_cached(key_buf, k * slots, refs[2 * k], refs[2 * k + 1])
    count = size // HEADS_STEP

    def scores(step):
        q = q_ref[span(step, size), :]
        return jnp.concatenate([dot_t(q, key_buf[span(k, slots), :]) for k in range(cached)], axis=1)

    def weigh(step, s):
        level = jnp.max(s, axis=1, keepdims=True)
        p, total = exponents(s, level, None)
        sum_ref[span(step, size), :] = total
        max_ref[span(step, size), :] = jnp.broadcast_to(level, (size, LANES))
        return (p,)

    def collect(step, p):
        mixed = dot(p, key_buf[:, :DC]).astype(BF16)
        if step == 0:
            copy.wait()
        for k in range(HEADS_STEP):
            head = step * HEADS_STEP + k
            out_ref[span(head, count), :] = dot(mixed[span(k, count), :], w_ref[:, span(head, DV)])

    pipeline(q_ref.shape[0] // size, scores, weigh, collect)


def near_pass(q, blocks, w_value, count):
    rows = q.shape[0]
    keys = sum(block[0].shape[0] for block in blocks)
    return pl.pallas_call(
        functools.partial(near_kernel, cached=len(blocks), size=HEADS_STEP * count),
        out_shape=(*state_shapes(rows), pltpu.VMEM(w_value.shape, BF16)),
        in_specs=[VMEM] * (1 + 2 * len(blocks)) + [HBM],
        out_specs=(VMEM, VMEM, VMEM, VMEM),
        scratch_shapes=[pltpu.VMEM((keys, KEY), BF16), pltpu.SemaphoreType.DMA],
        compiler_params=params(),
        cost_estimate=cost(COSTS["near_rows"]),
        name="near_rows",
    )(q, *[array for block in blocks for array in block], in_hbm(w_value))


def early_kernel(q_ref, lat_ref, w_ref, out_ref, value_ref, *, size):
    for step in range(q_ref.shape[0] // size):
        rows = span(step, size)
        out_ref[rows, :] = dot_t(q_ref[rows, :DC], lat_ref[...])
        cols = span(step, HEADS_STEP * DV)
        value_ref[:, cols] = dot(lat_ref[...], w_ref[:, cols]).astype(BF16)


def early_pass(q, lat, w_value, count):
    rows = q.shape[0]
    slots = lat.shape[0]
    return pl.pallas_call(
        functools.partial(early_kernel, size=HEADS_STEP * count),
        out_shape=(pltpu.VMEM((rows, slots), F32), pltpu.VMEM((slots, w_value.shape[1]), BF16)),
        in_specs=[VMEM] * 3,
        out_specs=(VMEM, VMEM),
        compiler_params=params(),
        cost_estimate=cost(COSTS["early"]),
        name="early",
    )(q, lat, w_value)


def far_kernel(
    q_ref,
    note_ref,
    s_ref,
    value_ref,
    out_in,
    sum_in,
    max_in,
    lat_ref,
    w_ref,
    out_ref,
    sum_ref,
    max_ref,
    next_ref,
    ext_buf,
    *,
    size,
):
    ext_buf[...] = masked_rope(note_ref, value_ref.shape[0])
    count = size // HEADS_STEP

    def scores(step):
        rows = span(step, size)
        return s_ref[rows, :] + dot_t(q_ref[rows, DC:], ext_buf[...])

    def weigh(step, s):
        rows = span(step, size)
        before = max_in[rows, :]
        level = jnp.maximum(before, jnp.max(s, axis=1, keepdims=True))
        factor = jnp.exp2((before - level) * EXP_SCALE)
        p, total = exponents(s, level, sum_in[rows, :] * factor)
        sum_ref[rows, :] = total
        max_ref[rows, :] = level
        cols = span(step, HEADS_STEP * DV)
        next_ref[:, cols] = dot(lat_ref[...], w_ref[:, cols]).astype(BF16)
        return p, factor

    def collect(step, p, factor):
        for k in range(HEADS_STEP):
            head = step * HEADS_STEP + k
            grown = dot(p[span(k, count), :], value_ref[:, span(head, DV)])
            out_ref[span(head, count), :] = out_in[span(head, count), :] * factor[span(k, count), :] + grown

    pipeline(q_ref.shape[0] // size, scores, weigh, collect)


def far_pass(q, note, scores, values, state, next_lat, w_value, count):
    rows = q.shape[0]
    return pl.pallas_call(
        functools.partial(far_kernel, size=HEADS_STEP * count),
        out_shape=(*state_shapes(rows), pltpu.VMEM((next_lat.shape[0], w_value.shape[1]), BF16)),
        in_specs=[VMEM] * 9,
        out_specs=(VMEM, VMEM, VMEM, VMEM),
        scratch_shapes=[pltpu.VMEM((values.shape[0], LANES), BF16)],
        compiler_params=params(),
        cost_estimate=cost(COSTS["far_rows"]),
        name="far_rows",
    )(q, note, scores, values, *state, next_lat, w_value)


def last_kernel(q_ref, lat_ref, value_ref, *refs, blocks, size):
    notes, refs = refs[:blocks], refs[blocks:]
    out_in, sum_in, max_in, w_ref, out_hbm, key_buf, out_buf, sems = refs
    slots = lat_ref.shape[0]
    count = out_hbm.shape[0]
    put_fresh(key_buf, slots, notes)
    put_cached(key_buf, 0, lat_ref, notes[-1])
    bias = jnp.concatenate([causal(count // blocks, blocks)] * HEADS_LAST, axis=0)
    copies = []

    def scores(step):
        q = q_ref[span(step, size), :]
        fresh = dot_t(q, key_buf[slots:, :]) + bias
        return jnp.concatenate([dot_t(q, key_buf[:slots, :]), fresh], axis=1)

    def weigh(step, s):
        rows = span(step, size)
        before = max_in[rows, :]
        level = jnp.maximum(before, jnp.max(s, axis=1, keepdims=True))
        factor = jnp.exp2((before - level) * EXP_SCALE)
        p, total = exponents(s, level, sum_in[rows, :] * factor)
        inverse = 1.0 / jnp.sum(total, axis=1, keepdims=True)
        fresh = dot(key_buf[slots:, :DC], w_ref[:, span(step, HEADS_LAST * DV)]).astype(BF16)
        return p, factor * inverse, inverse, fresh

    def collect(step, p, factor, inverse, fresh):
        for k in range(HEADS_LAST):
            head = step * HEADS_LAST + k
            part = span(k, count)
            grown = dot(p[part, :slots], value_ref[:, span(head, DV)]) + dot(p[part, slots:], fresh[:, span(k, DV)])
            whole = out_in[span(head, count), :] * factor[part, :] + grown * inverse[part, :]
            out_buf[:, span(head, DV)] = whole.astype(BF16)
            if head % HEADS_SENT == HEADS_SENT - 1:
                piece = head // HEADS_SENT
                cols = span(piece, HEADS_SENT * DV)
                copies.append(pltpu.make_async_copy(out_buf.at[:, cols], out_hbm.at[:, cols], sems.at[piece]))
                copies[-1].start()

    pipeline(q_ref.shape[0] // size, scores, weigh, collect)
    for copy in copies:
        copy.wait()


def last_pass(q, lat, values, notes, state, w_value, count):
    rows = q.shape[0]
    shape = (count, w_value.shape[1])
    return pl.pallas_call(
        functools.partial(last_kernel, blocks=len(notes), size=HEADS_LAST * count),
        out_shape=jax.ShapeDtypeStruct(shape, BF16),
        in_specs=[VMEM] * (7 + len(notes)),
        out_specs=HBM,
        scratch_shapes=[
            pltpu.VMEM((lat.shape[0] + count, KEY), BF16),
            pltpu.VMEM(shape, BF16),
            pltpu.SemaphoreType.DMA((rows // (HEADS_SENT * count),)),
        ],
        compiler_params=params(),
        cost_estimate=cost(COSTS["last_rows"]),
        name="last_rows",
    )(q, lat, values, *notes, *state, w_value)


def hop(array, bit):
    size = lax.axis_size("ctx")
    return lax.ppermute(array, "ctx", [(k, k ^ bit) for k in range(size)])


def shards(q_nope, q_rope, cache_latent, cache_rope, new_latent, new_rope, lengths, w_key, w_value):
    count = q_nope.shape[1]
    lat = cache_latent[0]
    far_lat, near_lat = hop(lat, 2), hop(lat, 1)
    heads = w_key.shape[1] // DH
    note, lat, own_q, own_r = pack(
        new_latent[0], new_rope[0], cache_rope[0].T, lat, q_nope, q_rope, lengths, heads
    )
    near_note = hop(note, 1)
    q = make_queries(own_q, own_r, w_key)
    far_note = hop(note, 2)
    *state, w_value = near_pass(q, [(lat, note), (near_lat, near_note)], w_value, count)
    last_lat = hop(after(far_lat, state[2]), 1)
    scores, values = early_pass(q, far_lat, w_value, count)
    last_note = hop(after(far_note, scores), 1)
    *state, values = far_pass(q, far_note, scores, values, state, last_lat, w_value, count)
    notes = [note, near_note, far_note, last_note]
    return last_pass(q, last_lat, values, notes, state, w_value, count)[None]


def solution(mesh):
    return jax.shard_map(
        shards,
        mesh=mesh,
        in_specs=(
            P("req", None, None),
            P("req", None, None),
            P("req", "ctx", None),
            P("req", "ctx", None),
            P("req", "ctx", None),
            P("req", "ctx", None),
            P("req", "ctx"),
            P(None, "ctx"),
            P(None, "ctx"),
        ),
        out_specs=P("req", None, "ctx"),
        check_vma=False,
    )
```

```python
import functools
import math

import jax
import jax.numpy as jnp
from jax import lax
from jax.experimental import pallas as pl
from jax.experimental.pallas import tpu as pltpu
from jax.sharding import PartitionSpec as P

DC = 512
DR = 64
DH = 128
DV = 128
LANES = 128
KEY = DC + LANES
BLOCKED = -1e30
EXP_SCALE = math.log2(math.e) / math.sqrt(DH + DR)
HEADS_STEP = 4
HEADS_LAST = 8
HEADS_SENT = 4
GROUP = 16
COSTS = {"pack": 0.6, "latent_queries": 0.001, "pass_on": 0.001, "near_rows": 1.0, "early": 3.0, "far_rows": 3.0, "last_rows": 0.001}
VMEM_LIMIT = 20 * 1024 * 1024


def cost(micros):
    return pl.CostEstimate(flops=int(micros * 1e9), bytes_accessed=1024, transcendentals=0)


BF16 = jnp.bfloat16
F32 = jnp.float32

VMEM = pl.BlockSpec(memory_space=pltpu.VMEM)
HBM = pl.BlockSpec(memory_space=pltpu.HBM)
ANYWHERE = pl.BlockSpec(memory_space=pl.ANY)


def iota(shape, dim):
    return lax.broadcasted_iota(jnp.int32, shape, dim)


def span(step, size, first=0):
    return slice(first + step * size, first + (step + 1) * size)


def params():
    return pltpu.CompilerParams(vmem_limit_bytes=VMEM_LIMIT)


def in_vmem(array):
    return pltpu.with_memory_space_constraint(array, pltpu.VMEM)


def dot(a, b):
    return jnp.dot(a, b, preferred_element_type=F32)


def dot_t(a, b):
    return lax.dot_general(a, b, (((1,), (1,)), ((), ())), preferred_element_type=F32)


def in_hbm(array):
    return pltpu.with_memory_space_constraint(array, pltpu.HBM)


def pack_kernel(
    fresh_hbm,
    rope_hbm,
    cached_hbm,
    lat_hbm,
    q_hbm,
    r_hbm,
    length_ref,
    note_ref,
    lat_ref,
    q_ref,
    r_ref,
    rope_buf,
    cached_buf,
    sems,
):
    part = fresh_hbm.shape[0]
    slots = cached_hbm.shape[1]
    me = lax.axis_index("ctx")
    q_first = pl.multiple_of(me * q_ref.shape[1], LANES)
    r_first = pl.multiple_of(me * r_ref.shape[1], LANES)
    pairs = [
        (rope_hbm, rope_buf),
        (cached_hbm, cached_buf),
        (fresh_hbm, note_ref.at[:part, :]),
        (q_hbm.at[0, :, pl.ds(q_first, q_ref.shape[1])], q_ref),
        (r_hbm.at[0, :, pl.ds(r_first, r_ref.shape[1])], r_ref),
        (lat_hbm, lat_ref),
    ]
    copies = [pltpu.make_async_copy(source, target, sems.at[k]) for k, (source, target) in enumerate(pairs)]
    for copy in copies:
        copy.start()
    groups = part // GROUP
    note_ref[part : part + GROUP, :] = jnp.zeros((GROUP, DC), BF16)
    live = jnp.broadcast_to(length_ref[...], (GROUP, LANES)).astype(F32).astype(BF16)
    note_ref[part : part + GROUP, groups * LANES : (groups + 1) * LANES] = live
    copies[0].wait()
    for k in range(groups):
        note_ref[part : part + GROUP, k * LANES : k * LANES + DR] = rope_buf[span(k, GROUP), :]
    copies[1].wait()
    note_ref[part + GROUP :, :slots] = cached_buf[: DR // 2, :]
    note_ref[part + GROUP :, slots:] = cached_buf[DR // 2 :, :]
    for copy in copies[2:]:
        copy.wait()


def pack(fresh, rope, cached_rope, lat, q_nope, q_rope, length, heads):
    part = fresh.shape[0]
    count = q_nope.shape[1]
    return pl.pallas_call(
        pack_kernel,
        out_shape=(
            pltpu.VMEM((part + GROUP + DR // 2, DC), BF16),
            pltpu.VMEM(lat.shape, BF16),
            pltpu.VMEM((count, heads * DH), BF16),
            pltpu.VMEM((count, heads * DR), BF16),
        ),
        in_specs=[HBM] * 6 + [VMEM],
        out_specs=(VMEM, VMEM, VMEM, VMEM),
        scratch_shapes=[
            pltpu.VMEM(rope.shape, BF16),
            pltpu.VMEM(cached_rope.shape, BF16),
            pltpu.SemaphoreType.DMA((6,)),
        ],
        compiler_params=params(),
        cost_estimate=cost(COSTS["pack"]),
        name="pack",
    )(*[in_hbm(array) for array in (fresh, rope, cached_rope, lat, q_nope, q_rope)], length)


def queries_kernel(q_ref, r_ref, w_ref, out_ref):
    count = q_ref.shape[0]
    heads = out_ref.shape[0] // count
    lane = iota((count, LANES), 1)
    side = jnp.where(lane == DR, 1.0, 0.0)
    for pair in range(heads // 2):
        both = r_ref[:, span(pair, LANES)].astype(F32)
        for odd in range(2):
            head = 2 * pair + odd
            one = pltpu.roll(both, DR, 1) if odd else both
            out_ref[span(head, count), :DC] = dot_t(q_ref[:, span(head, DH)], w_ref[:, span(head, DH)]).astype(BF16)
            out_ref[span(head, count), DC:] = jnp.where(lane < DR, one, side).astype(BF16)


def make_queries(q, r, w_key):
    count = q.shape[0]
    heads = w_key.shape[1] // DH
    return pl.pallas_call(
        queries_kernel,
        out_shape=pltpu.VMEM((heads * count, KEY), BF16),
        in_specs=[VMEM] * 3,
        out_specs=VMEM,
        compiler_params=params(),
        cost_estimate=cost(COSTS["latent_queries"]),
        name="latent_queries",
    )(q, r, in_vmem(w_key))


def pass_kernel(array_ref, token_ref, out_ref):
    out_ref[...] = array_ref[...]


def after(array, token):
    return pl.pallas_call(
        pass_kernel,
        out_shape=pltpu.VMEM(array.shape, BF16),
        in_specs=[VMEM, ANYWHERE],
        out_specs=VMEM,
        compiler_params=params(),
        cost_estimate=cost(COSTS["pass_on"]),
        name="pass_on",
    )(array, token)


def put_cached(key_buf, first, lat_ref, note_ref):
    slots = lat_ref.shape[0]
    key_buf[first : first + slots, :DC] = lat_ref[...]
    key_buf[first : first + slots, DC:] = masked_rope(note_ref, slots)


def masked_rope(note_ref, slots):
    part = note_ref.shape[0] - GROUP - DR // 2
    lane = part // GROUP * LANES
    live = note_ref[part : part + 1, lane : lane + 1].astype(F32)
    blocked = jnp.where(iota((LANES - DR, slots), 1).astype(F32) < live, 0.0, BLOCKED)
    blocked = jnp.where(iota((LANES - DR, slots), 0) == 0, blocked, 0.0)
    rope = note_ref[part + GROUP :, :].astype(F32)
    return jnp.concatenate([rope[:, :slots], rope[:, slots:], blocked], axis=0).T.astype(BF16)


def put_fresh(key_buf, first, note_refs):
    part = note_refs[0].shape[0] - GROUP - DR // 2
    for index, note_ref in enumerate(note_refs):
        key_buf[first + index * part : first + (index + 1) * part, :DC] = note_ref[:part, :]
        for k in range(part // GROUP):
            rows = span(k, GROUP, first + index * part)
            key_buf[rows, DC:] = note_ref[part : part + GROUP, k * LANES : (k + 1) * LANES]


def causal(part, blocks):
    count = part * blocks
    me = lax.axis_index("ctx")
    col = iota((count, count), 1)
    origin = jnp.bitwise_xor(jnp.full((count, count), me, jnp.int32), col // part)
    return jnp.where(origin * part + col % part <= iota((count, count), 0), 0.0, BLOCKED)


def pipeline(steps, scores, weigh, collect):
    upcoming, previous = scores(0), None
    for step in range(steps):
        now = upcoming
        if step + 1 < steps:
            upcoming = scores(step + 1)
        if previous is not None:
            collect(step - 1, *previous)
        previous = weigh(step, now)
    collect(steps - 1, *previous)


def exponents(s, level, total):
    parts = []
    for k in range(s.shape[1] // LANES):
        p = jnp.exp2((s[:, k * LANES : (k + 1) * LANES] - level) * EXP_SCALE)
        total = p if total is None else total + p
        parts.append(p.astype(BF16))
    return jnp.concatenate(parts, axis=1), total


def state_shapes(rows):
    return (pltpu.VMEM((rows, DV), F32), pltpu.VMEM((rows, LANES), F32), pltpu.VMEM((rows, LANES), F32))


def near_kernel(q_ref, *refs, cached, size):
    w_hbm, out_ref, sum_ref, max_ref, w_ref, key_buf, sem = refs[2 * cached :]
    copy = pltpu.make_async_copy(w_hbm, w_ref, sem)
    copy.start()
    slots = refs[0].shape[0]
    for k in range(cached):
        put_cached(key_buf, k * slots, refs[2 * k], refs[2 * k + 1])
    count = size // HEADS_STEP

    def scores(step):
        q = q_ref[span(step, size), :]
        return jnp.concatenate([dot_t(q, key_buf[span(k, slots), :]) for k in range(cached)], axis=1)

    def weigh(step, s):
        level = jnp.max(s, axis=1, keepdims=True)
        p, total = exponents(s, level, None)
        sum_ref[span(step, size), :] = total
        max_ref[span(step, size), :] = jnp.broadcast_to(level, (size, LANES))
        return (p,)

    def collect(step, p):
        mixed = dot(p, key_buf[:, :DC]).astype(BF16)
        if step == 0:
            copy.wait()
        for k in range(HEADS_STEP):
            head = step * HEADS_STEP + k
            out_ref[span(head, count), :] = dot(mixed[span(k, count), :], w_ref[:, span(head, DV)])

    pipeline(q_ref.shape[0] // size, scores, weigh, collect)


def near_pass(q, blocks, w_value, count):
    rows = q.shape[0]
    keys = sum(block[0].shape[0] for block in blocks)
    return pl.pallas_call(
        functools.partial(near_kernel, cached=len(blocks), size=HEADS_STEP * count),
        out_shape=(*state_shapes(rows), pltpu.VMEM(w_value.shape, BF16)),
        in_specs=[VMEM] * (1 + 2 * len(blocks)) + [HBM],
        out_specs=(VMEM, VMEM, VMEM, VMEM),
        scratch_shapes=[pltpu.VMEM((keys, KEY), BF16), pltpu.SemaphoreType.DMA],
        compiler_params=params(),
        cost_estimate=cost(COSTS["near_rows"]),
        name="near_rows",
    )(q, *[array for block in blocks for array in block], in_hbm(w_value))


def early_kernel(q_ref, lat_ref, w_ref, out_ref, value_ref, *, size):
    for step in range(q_ref.shape[0] // size):
        rows = span(step, size)
        out_ref[rows, :] = dot_t(q_ref[rows, :DC], lat_ref[...])
        cols = span(step, HEADS_STEP * DV)
        value_ref[:, cols] = dot(lat_ref[...], w_ref[:, cols]).astype(BF16)


def early_pass(q, lat, w_value, count):
    rows = q.shape[0]
    slots = lat.shape[0]
    return pl.pallas_call(
        functools.partial(early_kernel, size=HEADS_STEP * count),
        out_shape=(pltpu.VMEM((rows, slots), F32), pltpu.VMEM((slots, w_value.shape[1]), BF16)),
        in_specs=[VMEM] * 3,
        out_specs=(VMEM, VMEM),
        compiler_params=params(),
        cost_estimate=cost(COSTS["early"]),
        name="early",
    )(q, lat, w_value)


def far_kernel(
    q_ref,
    note_ref,
    s_ref,
    value_ref,
    out_in,
    sum_in,
    max_in,
    lat_ref,
    w_ref,
    out_ref,
    sum_ref,
    max_ref,
    next_ref,
    ext_buf,
    *,
    size,
):
    ext_buf[...] = masked_rope(note_ref, value_ref.shape[0])
    count = size // HEADS_STEP

    def scores(step):
        rows = span(step, size)
        return s_ref[rows, :] + dot_t(q_ref[rows, DC:], ext_buf[...])

    def weigh(step, s):
        rows = span(step, size)
        before = max_in[rows, :]
        level = jnp.maximum(before, jnp.max(s, axis=1, keepdims=True))
        factor = jnp.exp2((before - level) * EXP_SCALE)
        p, total = exponents(s, level, sum_in[rows, :] * factor)
        sum_ref[rows, :] = total
        max_ref[rows, :] = level
        cols = span(step, HEADS_STEP * DV)
        next_ref[:, cols] = dot(lat_ref[...], w_ref[:, cols]).astype(BF16)
        return p, factor

    def collect(step, p, factor):
        for k in range(HEADS_STEP):
            head = step * HEADS_STEP + k
            grown = dot(p[span(k, count), :], value_ref[:, span(head, DV)])
            out_ref[span(head, count), :] = out_in[span(head, count), :] * factor[span(k, count), :] + grown

    pipeline(q_ref.shape[0] // size, scores, weigh, collect)


def far_pass(q, note, scores, values, state, next_lat, w_value, count):
    rows = q.shape[0]
    return pl.pallas_call(
        functools.partial(far_kernel, size=HEADS_STEP * count),
        out_shape=(*state_shapes(rows), pltpu.VMEM((next_lat.shape[0], w_value.shape[1]), BF16)),
        in_specs=[VMEM] * 9,
        out_specs=(VMEM, VMEM, VMEM, VMEM),
        scratch_shapes=[pltpu.VMEM((values.shape[0], LANES), BF16)],
        compiler_params=params(),
        cost_estimate=cost(COSTS["far_rows"]),
        name="far_rows",
    )(q, note, scores, values, *state, next_lat, w_value)


def last_kernel(q_ref, lat_ref, value_ref, *refs, blocks, size):
    notes, refs = refs[:blocks], refs[blocks:]
    out_in, sum_in, max_in, w_ref, out_hbm, key_buf, out_buf, sems = refs
    slots = lat_ref.shape[0]
    count = out_hbm.shape[0]
    put_fresh(key_buf, slots, notes)
    put_cached(key_buf, 0, lat_ref, notes[-1])
    bias = jnp.concatenate([causal(count // blocks, blocks)] * HEADS_LAST, axis=0)
    copies = []

    def scores(step):
        q = q_ref[span(step, size), :]
        fresh = dot_t(q, key_buf[slots:, :]) + bias
        return jnp.concatenate([dot_t(q, key_buf[:slots, :]), fresh], axis=1)

    def weigh(step, s):
        rows = span(step, size)
        before = max_in[rows, :]
        level = jnp.maximum(before, jnp.max(s, axis=1, keepdims=True))
        factor = jnp.exp2((before - level) * EXP_SCALE)
        p, total = exponents(s, level, sum_in[rows, :] * factor)
        inverse = 1.0 / jnp.sum(total, axis=1, keepdims=True)
        fresh = dot(key_buf[slots:, :DC], w_ref[:, span(step, HEADS_LAST * DV)]).astype(BF16)
        return p, factor * inverse, inverse, fresh

    def collect(step, p, factor, inverse, fresh):
        for k in range(HEADS_LAST):
            head = step * HEADS_LAST + k
            part = span(k, count)
            grown = dot(p[part, :slots], value_ref[:, span(head, DV)]) + dot(p[part, slots:], fresh[:, span(k, DV)])
            whole = out_in[span(head, count), :] * factor[part, :] + grown * inverse[part, :]
            out_buf[:, span(head, DV)] = whole.astype(BF16)
            if head % HEADS_SENT == HEADS_SENT - 1:
                piece = head // HEADS_SENT
                cols = span(piece, HEADS_SENT * DV)
                copies.append(pltpu.make_async_copy(out_buf.at[:, cols], out_hbm.at[:, cols], sems.at[piece]))
                copies[-1].start()

    pipeline(q_ref.shape[0] // size, scores, weigh, collect)
    for copy in copies:
        copy.wait()


def last_pass(q, lat, values, notes, state, w_value, count):
    rows = q.shape[0]
    shape = (count, w_value.shape[1])
    return pl.pallas_call(
        functools.partial(last_kernel, blocks=len(notes), size=HEADS_LAST * count),
        out_shape=jax.ShapeDtypeStruct(shape, BF16),
        in_specs=[VMEM] * (7 + len(notes)),
        out_specs=HBM,
        scratch_shapes=[
            pltpu.VMEM((lat.shape[0] + count, KEY), BF16),
            pltpu.VMEM(shape, BF16),
            pltpu.SemaphoreType.DMA((rows // (HEADS_SENT * count),)),
        ],
        compiler_params=params(),
        cost_estimate=cost(COSTS["last_rows"]),
        name="last_rows",
    )(q, lat, values, *notes, *state, w_value)


def hop(array, bit):
    size = lax.axis_size("ctx")
    return lax.ppermute(array, "ctx", [(k, k ^ bit) for k in range(size)])


def shards(q_nope, q_rope, cache_latent, cache_rope, new_latent, new_rope, lengths, w_key, w_value):
    count = q_nope.shape[1]
    lat = cache_latent[0]
    far_lat, near_lat = hop(lat, 2), hop(lat, 1)
    heads = w_key.shape[1] // DH
    note, lat, own_q, own_r = pack(
        new_latent[0], new_rope[0], cache_rope[0].T, lat, q_nope, q_rope, lengths, heads
    )
    near_note = hop(note, 1)
    q = make_queries(own_q, own_r, w_key)
    far_note = hop(note, 2)
    *state, w_value = near_pass(q, [(lat, note), (near_lat, near_note)], w_value, count)
    last_lat = hop(after(far_lat, state[2]), 1)
    scores, values = early_pass(q, far_lat, w_value, count)
    last_note = hop(after(far_note, scores), 1)
    *state, values = far_pass(q, far_note, scores, values, state, last_lat, w_value, count)
    notes = [note, near_note, far_note, last_note]
    return last_pass(q, last_lat, values, notes, state, w_value, count)[None]


def solution(mesh):
    return jax.shard_map(
        shards,
        mesh=mesh,
        in_specs=(
            P("req", None, None),
            P("req", None, None),
            P("req", "ctx", None),
            P("req", "ctx", None),
            P("req", "ctx", None),
            P("req", "ctx", None),
            P("req", "ctx"),
            P(None, "ctx"),
            P(None, "ctx"),
        ),
        out_specs=P("req", None, "ctx"),
        check_vma=False,
    )
```
